32 devices in a mesh: fsdp: 4 (over z), expert: 8 (over y, x, core).
Axes of the slice: x: 2, y: 2, z: 4, core: 2. Of those that a mesh axis runs over, the one named last changes fastest.
Arguments:
- tokens: bfloat16 [16384, 2048], P(('fsdp', 'expert')), may hold values from -6 to 6
- segments: int32 [32, 512], P(('fsdp', 'expert')), may hold values from 0 to 5, never falling along the last dimension, each value on 1 to 256 neighbouring positions
- routes: int32 [16384, 8], P(('fsdp', 'expert')), may hold values from 0 to 31, as said below
- w_query: bfloat16 [2048, 4096], P('fsdp'), may hold values from -0.125 to 0.125
- key_projection: bfloat16 [2048, 512], P('fsdp'), may hold values from -0.125 to 0.125
- value_projection: bfloat16 [2048, 512], P('fsdp'), may hold values from -0.125 to 0.125
- w_out: bfloat16 [4096, 2048], P('fsdp'), may hold values from -0.75 to 0.75
- w_router: bfloat16 [2048, 32], P('fsdp'), may hold values from -0.0625 to 0.0625
- gain_attn: bfloat16 [2048], P('fsdp'), may hold values from 0.5 to 1.5
- gain_ffn: bfloat16 [2048], P('fsdp'), may hold values from 0.5 to 1.5
- gain_query: bfloat16 [128], P('fsdp'), may hold values from 0.25 to 1.75
- key_head_gain: bfloat16 [128], P('fsdp'), may hold values from 0.25 to 1.75
- w_gate: bfloat16 [32, 2048, 768], P(('fsdp', 'expert')), may hold values from -0.125 to 0.125
- w_up: bfloat16 [32, 2048, 768], P(('fsdp', 'expert')), may hold values from -0.125 to 0.125
- w_down: bfloat16 [32, 768, 2048], P(('fsdp', 'expert')), may hold values from -1.25 to 1.25
- cotangent: bfloat16 [16384, 2048], P(('fsdp', 'expert')), may hold values from -6 to 6
Outputs:
- output: bfloat16 [16384, 2048], P(('fsdp', 'expert'))
- d_tokens: bfloat16 [16384, 2048], P(('fsdp', 'expert'))
- d_w_query: float32 [2048, 4096], P('fsdp')
- d_w_key: float32 [2048, 512], P('fsdp')
- d_w_value: float32 [2048, 512], P('fsdp')
- d_w_out: float32 [4096, 2048], P('fsdp')
- d_w_router: float32 [2048, 32], P('fsdp')
- d_gain_attn: float32 [2048], P('fsdp')
- d_gain_ffn: float32 [2048], P('fsdp')
- d_gain_query: float32 [128], P('fsdp')
- d_gain_key: float32 [128], P('fsdp')
- d_w_gate: float32 [32, 2048, 768], P(('fsdp', 'expert'))
- d_w_up: float32 [32, 2048, 768], P(('fsdp', 'expert'))
- d_w_down: float32 [32, 768, 2048], P(('fsdp', 'expert'))
The draws below stay inside these ranges and needn't reach their ends.
Inputs may be any that keep to these rules, and one draw needn't show every extreme that they name: `routes`: each row names 8 different experts. In the rows of one device no expert is named more than 160 times; 8 experts, drawn from the seed, are named exactly 160 times in the rows of every device.
All inputs are finite; a program needn't handle non-finite values.
Results may differ from the reference program's by a relative error of at most 0.022.
Values may be sent and summed in bfloat16 or wider, within the bound.
A program may use at most 512 MiB of HBM per device.

```python
import math
import jax
import jax.numpy as jnp
import numpy as np
from jax import lax

MODEL_WIDTH = 2048
QUERY_HEADS = 32
KEY_VALUE_HEADS = 4
HEAD_SIZE = 128
FF = 768
TOP = 8
DEVICE_TOKENS = 512
EXPERTS = 32
TOKENS = 16384
SEQS = 32
CAP = 160


def draw_routes(key, part):
    key = jax.random.fold_in(key, 7)
    quarter = EXPERTS // 4
    spread = DEVICE_TOKENS * TOP // EXPERTS // 4
    blocks = TOKENS // DEVICE_TOKENS
    common = jax.random.permutation(jax.random.fold_in(key, 1), EXPERTS).astype(jnp.int32)
    block_keys = jax.random.split(jax.random.fold_in(key, 2), blocks)
    slot_index = jnp.arange(DEVICE_TOKENS, dtype=jnp.int32)[:, None] + DEVICE_TOKENS * jnp.arange(TOP, dtype=jnp.int32)[None, :]

    def one_block(block_key):
        key_order, key_first, key_second = jax.random.split(block_key, 3)
        shuffled = jax.random.permutation(key_order, 3 * quarter)
        expert_order = jnp.concatenate([common[:quarter], common[quarter:][shuffled]])
        first_shift = jax.random.randint(key_first, (quarter,), 0, spread + 1).astype(jnp.int32)
        second_shift = jax.random.randint(key_second, (quarter,), 0, spread + 1).astype(jnp.int32)
        block_loads = jnp.concatenate([jnp.full((quarter,), CAP, jnp.int32), 3 * spread + first_shift, 4 * spread - first_shift + second_shift, 4 * spread - second_shift])
        load_ends = jnp.cumsum(block_loads.astype(jnp.int32)).astype(jnp.int32)
        position = jnp.searchsorted(load_ends, slot_index, side='right')
        return expert_order[position]
    return jax.vmap(one_block)(block_keys).reshape(TOKENS, TOP).astype(jnp.int32)


def block_levels(stream_key, dims, cuts, low, top_value):
    def one(dim, shards_of):
        heights = jax.random.uniform(jax.random.fold_in(jax.random.fold_in(stream_key, 6), dim), (shards_of,), jnp.float32, low / len(cuts), top_value / len(cuts))
        return jnp.repeat(jnp.exp(heights), dims[dim] // shards_of).reshape((-1,) + (1,) * (len(dims) - dim - 1))

    level = one(*cuts[0])
    for cut in cuts[1:]:
        level = level * one(*cut)
    return level


def split_up(number_of, total, bound, lean):
    loads = [(1 << 20) // math.isqrt(grade ** lean) + 1 for grade in range(2, number_of + 1)]
    rest, counts = total - bound - (number_of - 1), [1] * (number_of - 1)
    while rest > 0:
        candidates = [i for i in range(number_of - 1) if counts[i] < bound]
        mass, budget = sum([loads[i] for i in candidates]), rest
        for i in candidates:
            extra = min(bound - counts[i], max(1, budget * loads[i] // mass), rest)
            counts[i] = counts[i] + extra
            rest = rest - extra
    return np.array([bound] + counts)


def uneven(stream_key, number_of, total, limit, slope):
    if number_of == 2:
        one = jax.random.randint(stream_key, (), max(1, total - limit), min(limit, total - 1) + 1)
        return jnp.stack([one, total - one])
    tallies = jnp.asarray(split_up(number_of, total, limit, slope), jnp.int32)
    twos = (number_of - 1) // 2
    donor, taker = tallies[1:1 + 2 * twos:2], tallies[2:2 + 2 * twos:2]
    margin = jnp.minimum(donor - 1, limit - taker)
    shifted = jax.random.randint(jax.random.fold_in(stream_key, 1), (twos,), 0, 1 << 20) % (margin + 1)
    tallies = tallies.at[1:1 + 2 * twos:2].set(donor - shifted).at[2:2 + 2 * twos:2].set(taker + shifted)
    return tallies[jax.random.permutation(jax.random.fold_in(stream_key, 2), number_of)]


def centred(own_key, shape, scale, bound, cuts=(), held_as=jnp.bfloat16):
    values = scale * jax.random.normal(own_key, shape, jnp.float32)
    if cuts:
        values = values * block_levels(own_key, shape, cuts, -0.22, 0.18)
    return jnp.clip(values, -bound, bound).astype(held_as)


def setup_inputs(seed: int = 0) -> dict:
    seeds = jax.random.split(jax.random.key(seed), 17)
    tokens = centred(seeds[0], (TOKENS, MODEL_WIDTH), 1.0, 6.0, ((0, 32),))
    segments = jax.vmap(lambda own: jnp.searchsorted(jnp.cumsum(uneven(own, 6, DEVICE_TOKENS, DEVICE_TOKENS // 2, 2)), jnp.arange(DEVICE_TOKENS), side="right"))(jax.random.split(seeds[1], SEQS)).reshape((SEQS, DEVICE_TOKENS)).astype(jnp.int32)
    routes = draw_routes(jax.random.fold_in(seeds[16], 71), 0)
    w_query = centred(seeds[3], (MODEL_WIDTH, QUERY_HEADS * HEAD_SIZE), MODEL_WIDTH ** -0.5, 0.125, ((0, 4),))
    key_projection = centred(seeds[4], (MODEL_WIDTH, KEY_VALUE_HEADS * HEAD_SIZE), MODEL_WIDTH ** -0.5, 0.125, ((0, 4),))
    value_projection = centred(seeds[5], (MODEL_WIDTH, KEY_VALUE_HEADS * HEAD_SIZE), MODEL_WIDTH ** -0.5, 0.125, ((0, 4),))
    w_out = centred(seeds[6], (QUERY_HEADS * HEAD_SIZE, MODEL_WIDTH), (QUERY_HEADS * HEAD_SIZE // 64) ** -0.5, 0.75, ((0, 4),))
    w_router = centred(seeds[7], (MODEL_WIDTH, EXPERTS), (4 * MODEL_WIDTH) ** -0.5, 0.0625, ((0, 4),))
    gain_attn = jnp.clip(1.0 + 0.1 * jax.random.normal(seeds[8], (MODEL_WIDTH,), jnp.float32), 0.5, 1.5).astype(jnp.bfloat16)
    gain_ffn = jnp.clip(1.0 + 0.1 * jax.random.normal(seeds[9], (MODEL_WIDTH,), jnp.float32), 0.5, 1.5).astype(jnp.bfloat16)
    gain_query = jnp.clip(1.0 + 0.15 * jax.random.normal(seeds[10], (HEAD_SIZE,), jnp.float32), 0.25, 1.75).astype(jnp.bfloat16)
    key_head_gain = jnp.clip(1.0 + 0.15 * jax.random.normal(seeds[11], (HEAD_SIZE,), jnp.float32), 0.25, 1.75).astype(jnp.bfloat16)
    w_gate = centred(seeds[12], (EXPERTS, MODEL_WIDTH, FF), MODEL_WIDTH ** -0.5, 0.125, ((0, 32),))
    w_up = centred(seeds[13], (EXPERTS, MODEL_WIDTH, FF), MODEL_WIDTH ** -0.5, 0.125, ((0, 32),))
    w_down = centred(seeds[14], (EXPERTS, FF, MODEL_WIDTH), (FF // 32) ** -0.5, 1.25, ((0, 32),))
    cotangent = centred(seeds[15], (TOKENS, MODEL_WIDTH), 1.0, 6.0, ((0, 32),))
    return {"tokens": tokens, "segments": segments, "routes": routes, "w_query": w_query, "key_projection": key_projection, "value_projection": value_projection, "w_out": w_out, "w_router": w_router, "gain_attn": gain_attn, "gain_ffn": gain_ffn, "gain_query": gain_query, "key_head_gain": key_head_gain, "w_gate": w_gate, "w_up": w_up, "w_down": w_down, "cotangent": cotangent}


EPSILON = 1e-06
ROPE_BASE = 1000000.0
HIGHEST_PRECISION = lax.Precision.HIGHEST

@jax.custom_vjp
def reduced_input(v):
    return lax.optimization_barrier(v.astype(jnp.bfloat16)).astype(jnp.float32)

@jax.custom_vjp
def reduced_gradient(v):
    return v

def low_keep(v):
    return (reduced_input(v), None)

def low_pass(kept, grad):
    return (grad,)

def back_keep(v):
    return (v, None)

def back_low(kept, grad):
    return (reduced_input(grad),)
reduced_input.defvjp(low_keep, low_pass)
reduced_gradient.defvjp(back_keep, back_low)

def projected_product(left_in, right_in):
    return jnp.dot(left_in, right_in, precision=HIGHEST_PRECISION)

def root_mean_norm(values_in, gain_in):
    return values_in * lax.rsqrt(lax.optimization_barrier(jnp.mean(values_in * values_in, axis=-1, keepdims=True)) + EPSILON) * gain_in

def rope_tables(sequence_length, width):
    inverse = 1.0 / ROPE_BASE ** (jnp.arange(0, width, 2, dtype=jnp.float32) / width)
    angles = jnp.arange(sequence_length, dtype=jnp.float32)[:, None] * inverse[None, :]
    angles = jnp.concatenate([angles, angles], axis=-1)
    return (jnp.cos(angles)[:, None, :], jnp.sin(angles)[:, None, :])

def rotary_apply(values_in, cosine_table, sine_values):
    half_width = values_in.shape[-1] // 2
    turned = jnp.concatenate([-values_in[..., half_width:], values_in[..., :half_width]], axis=-1)
    return values_in * cosine_table + turned * sine_values

def attend(inputs_tuple):
    query_input, key_input, value_in, seg_row = inputs_tuple
    sequence_length = query_input.shape[0]
    grouped_heads = query_input.reshape(sequence_length, KEY_VALUE_HEADS, QUERY_HEADS // KEY_VALUE_HEADS, HEAD_SIZE)
    scores = jnp.einsum('sjgd,tjd->jgst', grouped_heads, key_input, precision=HIGHEST_PRECISION) * HEAD_SIZE ** (-0.5)
    scores = reduced_gradient(scores)
    position = jnp.arange(sequence_length)
    allowed = (seg_row[:, None] == seg_row[None, :]) & (position[None, :] <= position[:, None])
    weights = reduced_input(jax.nn.softmax(jnp.where(allowed, scores, -1e+30), axis=-1))
    mixed = jnp.einsum('jgst,tjd->sjgd', weights, value_in, precision=HIGHEST_PRECISION)
    return mixed.reshape(sequence_length, QUERY_HEADS * HEAD_SIZE)

def forward_layer(inputs, seg_rows, routes, token_of, slot_place, w_query, key_projection, value_projection, w_out, w_router, gain_attn, gain_ffn, gain_query, key_head_gain, w_gate, w_up, w_down):
    total_count = inputs.shape[0]
    packed_sequences = total_count // DEVICE_TOKENS
    normalized = reduced_input(root_mean_norm(inputs, gain_attn))
    query = reduced_gradient(projected_product(normalized, w_query)).reshape(total_count, QUERY_HEADS, HEAD_SIZE)
    key_head_rows = reduced_gradient(projected_product(normalized, key_projection)).reshape(total_count, KEY_VALUE_HEADS, HEAD_SIZE)
    value_head_rows = reduced_input(reduced_gradient(projected_product(normalized, value_projection))).reshape(packed_sequences, DEVICE_TOKENS, KEY_VALUE_HEADS, HEAD_SIZE)
    cosine_table, sine_values = rope_tables(DEVICE_TOKENS, HEAD_SIZE)
    query = reduced_input(rotary_apply(root_mean_norm(query, gain_query).reshape(packed_sequences, DEVICE_TOKENS, QUERY_HEADS, HEAD_SIZE), cosine_table, sine_values))
    key_head_rows = reduced_input(rotary_apply(root_mean_norm(key_head_rows, key_head_gain).reshape(packed_sequences, DEVICE_TOKENS, KEY_VALUE_HEADS, HEAD_SIZE), cosine_table, sine_values))
    mixed = lax.map(jax.checkpoint(attend), (query, key_head_rows, value_head_rows, seg_rows)).reshape(total_count, QUERY_HEADS * HEAD_SIZE)
    mixed = reduced_gradient(reduced_input(mixed))
    hidden = inputs + reduced_gradient(projected_product(mixed, w_out))
    routed = reduced_input(root_mean_norm(hidden, gain_ffn))
    router = jax.nn.softmax(reduced_gradient(projected_product(routed, w_router)), axis=-1)
    chosen = jnp.take_along_axis(router, routes, axis=1)
    gates = chosen / lax.optimization_barrier(jnp.sum(chosen, axis=-1, keepdims=True))
    padded = jnp.concatenate([routed, jnp.zeros((1, routed.shape[1]), routed.dtype)], axis=0)

    def expert(inputs_tuple):
        index_rows, gate_weight, up_weight, down_weight = inputs_tuple
        rows_in = reduced_gradient(padded[index_rows])
        gate_part = reduced_gradient(projected_product(rows_in, gate_weight))
        up_part = reduced_gradient(projected_product(rows_in, up_weight))
        activation = reduced_input(jax.nn.silu(gate_part) * up_part)
        return reduced_gradient(reduced_input(projected_product(activation, down_weight)))
    results = lax.map(jax.checkpoint(expert), (token_of, w_gate, w_up, w_down))
    results = results.reshape(-1, results.shape[-1])
    combined = hidden
    for pick_index in range(TOP):
        combined = combined + gates[:, pick_index:pick_index + 1] * results[slot_place[:, pick_index]]
    return combined

def reference(tokens, segments, routes, w_query, key_projection, value_projection, w_out, w_router, gain_attn, gain_ffn, gain_query, key_head_gain, w_gate, w_up, w_down, cotangent):
    total_count = routes.shape[0]
    experts = w_gate.shape[0]
    capacity = total_count // DEVICE_TOKENS * CAP
    flat_routes = routes.reshape(-1).astype(jnp.int32)
    route_hits = (flat_routes[:, None] == jnp.arange(experts, dtype=jnp.int32)[None, :]).astype(jnp.int32)
    route_rank = lax.optimization_barrier(jnp.sum((jnp.cumsum(route_hits, axis=0).astype(jnp.int32) - 1) * route_hits, axis=1)).astype(jnp.int32)
    slot_place = (flat_routes * capacity + route_rank).astype(jnp.int32)
    token_ids = (jnp.arange(total_count * TOP, dtype=jnp.int32) // TOP).astype(jnp.int32)
    token_of = jnp.full((experts * capacity,), total_count, jnp.int32).at[slot_place].set(token_ids)
    token_of = token_of.reshape(experts, capacity).astype(jnp.int32)
    slot_place = slot_place.reshape(total_count, TOP)
    floats = [array.astype(jnp.float32) for array in (tokens, w_query, key_projection, value_projection, w_out, w_router, gain_attn, gain_ffn, gain_query, key_head_gain, w_gate, w_up, w_down)]

    def run_layer(*values):
        return forward_layer(values[0], segments, routes, token_of, slot_place, *values[1:])
    result, pull_back = jax.vjp(run_layer, *floats)
    grads = pull_back(cotangent.astype(jnp.float32))
    return (result.astype(jnp.bfloat16), grads[0].astype(jnp.bfloat16), grads[1], grads[2], grads[3], grads[4], grads[5], grads[6], grads[7], grads[8], grads[9], grads[10], grads[11], grads[12])
```

```python
import functools

import jax
import jax.numpy as jnp
from jax import lax
from jax.experimental import pallas as pl
from jax.experimental.pallas import tpu as pltpu
from jax.sharding import PartitionSpec as P

MODEL_WIDTH = 2048
QUERY_HEADS = 32
KEY_VALUE_HEADS = 4
HEAD_SIZE = 128
TOP = 8
DEVICE_TOKENS = 512


EPSILON = 1e-06
ROPE_BASE = 1000000.0


def root_mean_norm(values_in, gain_in):
    return (
        values_in
        * lax.rsqrt(jnp.mean(values_in * values_in, axis=-1, keepdims=True) + EPSILON)
        * gain_in
    )


def rope_tables(sequence_length, width):
    inverse = 1.0 / ROPE_BASE ** (jnp.arange(0, width, 2, dtype=jnp.float32) / width)
    angles = jnp.arange(sequence_length, dtype=jnp.float32)[:, None] * inverse[None, :]
    cosine, sine = jnp.cos(angles), jnp.sin(angles)
    return (
        jnp.concatenate([cosine, cosine], axis=-1),
        jnp.concatenate([-sine, sine], axis=-1),
    )


def swiglu(gate_in, up_in):
    return jax.nn.silu(gate_in) * up_in


BOTH = ("fsdp", "expert")


def gather_shards(shard):
    parts = lax.axis_size("expert")
    rows = shard.shape[0] // parts
    own = lax.dynamic_slice_in_dim(shard, lax.axis_index("expert") * rows, rows, axis=0)
    return lax.all_gather(own, BOTH, axis=0, tiled=True)


def scatter_sums(whole):
    part = lax.psum_scatter(whole, BOTH, scatter_dimension=0, tiled=True)
    return lax.all_gather(part, "expert", axis=0, tiled=True).astype(jnp.float32)


def routed_weight_grads(rows, gate_low, up_low):
    return tuple(
        jnp.einsum("rd,rf->df", rows, low, preferred_element_type=jnp.float32)
        for low in (gate_low, up_low)
    )


def down_weight_grads(row_cotangent, act_scaled):
    return jnp.einsum(
        "rf,rd->fd", act_scaled, row_cotangent, preferred_element_type=jnp.float32
    )


def expert_layer(rows, row_cotangent, row_gates, w_gate, w_up, w_down):
    f32 = jnp.float32
    low = jnp.bfloat16
    gate_part = jnp.dot(rows, w_gate, preferred_element_type=f32)
    up_part = jnp.dot(rows, w_up, preferred_element_type=f32)
    activation, swiglu_back = jax.vjp(swiglu, gate_part, up_part)
    act_low = activation.astype(low)
    out_rows = (
        jnp.dot(act_low, w_down, preferred_element_type=f32) * row_gates[:, None]
    ).astype(low)
    act_pull = jnp.einsum("rd,fd->rf", row_cotangent, w_down, preferred_element_type=f32)
    gate_grad = jnp.sum(act_low.astype(f32) * act_pull, axis=-1)
    act_scaled = (act_low.astype(f32) * row_gates[:, None]).astype(low)
    gate_part_grad, up_part_grad = swiglu_back(act_pull * row_gates[:, None])
    gate_low = gate_part_grad.astype(low)
    up_low = up_part_grad.astype(low)
    rows_grad = (
        jnp.einsum("rf,df->rd", gate_low, w_gate, preferred_element_type=f32)
        + jnp.einsum("rf,df->rd", up_low, w_up, preferred_element_type=f32)
    ).astype(low)
    weight_grads = routed_weight_grads(rows, gate_low, up_low)
    weight_grads += (down_weight_grads(row_cotangent, act_scaled),)
    return (out_rows, rows_grad, gate_grad) + weight_grads


def ranks(hits):
    length = hits.shape[-1]
    before = jnp.arange(length)[:, None] <= jnp.arange(length)[None, :]
    counts = jnp.einsum(
        "...s,st->...t",
        hits.astype(jnp.bfloat16),
        before.astype(jnp.bfloat16),
        preferred_element_type=jnp.float32,
    )
    return jnp.where(hits, counts.astype(jnp.int32) - 1, -1)


def places(hits, capacity):
    slots = jnp.arange(capacity, dtype=jnp.int32)
    return (ranks(hits)[..., None, :] == slots[:, None]).astype(jnp.bfloat16)


MESH = pl.DeviceIdType.MESH
LINE = 4
PLANE = 8
PART = 512
FAR_FIRST = (3, 0, 2, 1)


class Place:
    def __init__(self):
        self.z = lax.axis_index("fsdp")
        self.e = lax.axis_index("expert")
        core = lax.rem(self.e, 2)
        x = lax.rem(lax.div(self.e, 2), 2)
        y = lax.div(self.e, 4)
        self.sib = self.e + 1 - 2 * core
        self.x_same = self.e + 2 - 4 * x
        self.y_same = self.e + 4 - 8 * y
        self.d_same = self.x_same + 4 - 8 * y
        self.x_other = self.x_same + 1 - 2 * core
        self.y_other = self.y_same + 1 - 2 * core
        self.d_other = self.d_same + 1 - 2 * core
        self.plane = [lax.rem(self.e + k, PLANE) for k in range(1, PLANE)]
        self.line = [lax.rem(self.z + k, LINE) for k in range(1, LINE)]

    def greet(self):
        barrier = pltpu.get_barrier_semaphore()
        others = [(self.z, other) for other in self.plane] + [(other, self.e) for other in self.line]
        for z, e in others:
            pl.semaphore_signal(barrier, inc=1, device_id=(z, e), device_id_type=MESH)
        pl.semaphore_wait(barrier, len(others))


def push(source, target, send, recv, z, e):
    return pltpu.make_async_remote_copy(
        src_ref=source,
        dst_ref=target,
        send_sem=send,
        recv_sem=recv,
        device_id=(z, e),
        device_id_type=MESH,
    )


def part_columns(half, part):
    return pl.ds(half * 2 * PART + part * PART, PART)


def one_hot(pos_ref, experts, block, capacity):
    slots = lax.broadcasted_iota(jnp.int32, (capacity, DEVICE_TOKENS), 0)
    return jnp.concatenate(
        [
            (slots == pos_ref[expert, pl.ds(block, 1), :]).astype(jnp.float32)
            for expert in experts
        ],
        axis=0,
    ).astype(jnp.bfloat16)


def along_line(here, source, goal, send, recv):
    return [
        push(
            source.at[plane],
            goal.at[here.z],
            send.at[k],
            recv.at[here.z],
            plane,
            here.e,
        )
        for k, plane in enumerate(here.line)
    ]


def in_plane_of(here, source, goal, send, recv):
    return [
        push(
            source.at[:, owner],
            goal.at[:, here.e],
            send.at[k],
            recv.at[here.e],
            here.z,
            owner,
        )
        for k, owner in enumerate(here.plane)
    ]


def target_sets(here):
    with_y = (here.e, here.sib, here.y_same, here.y_other)
    with_x = (here.e, here.sib, here.x_same, here.x_other)
    return (
        (here.e, 0, with_y),
        (here.e, 1, with_x),
        (here.x_same, 0, with_y),
        (here.y_same, 1, with_x),
    )


CUTS = 4
CUT = 256
AHEAD = 2


def cut_columns(half, part):
    return pl.ds(half * CUTS * CUT + part * CUT, CUT)


def combine_kernel(
    pos_ref,
    gate_grad_ref,
    rows_ref,
    out_ref,
    gate_out_ref,
    gates_plane,
    held,
    dense_out,
    dense_in,
    sums,
    passed,
    held_send,
    held_recv,
    dense_send,
    dense_recv,
    pass_send,
    pass_recv,
    gate_plane_send,
    gate_plane_recv,
    gate_line_send,
    gate_line_recv,
):
    here = Place()
    z, e = here.z, here.e
    capacity = rows_ref.shape[1]
    here.greet()
    targets = target_sets(here)
    units = [(part, plane) for part in range(CUTS) for plane in FAR_FIRST]
    at_end = []

    def unit_of(part, plane):
        return part * LINE + plane

    def compact(index):
        part, plane = units[index]
        unit = unit_of(part, plane)

        def rows_of(owner, half):
            return rows_ref.at[plane * PLANE + owner, :, cut_columns(half, part)]

        def slot(number, k):
            return held.at[unit, number, pl.ds(k * capacity, capacity)]

        for number, owner, half in (
            (2, here.x_same, 0),
            (3, here.y_same, 1),
            (0, here.e, 0),
            (1, here.e, 1),
        ):
            pltpu.make_async_copy(
                rows_of(owner, half), slot(number, 0), held_recv.at[unit, number, 0]
            ).start()
        for count, (goal, number, k, owner, half) in enumerate(
            (
                (here.y_same, 2, 2, here.d_same, 0),
                (here.x_same, 3, 2, here.d_same, 1),
                (here.y_other, 2, 3, here.d_other, 0),
                (here.x_other, 3, 3, here.d_other, 1),
                (here.sib, 2, 1, here.x_other, 0),
                (here.sib, 3, 1, here.y_other, 1),
                (here.sib, 0, 1, here.sib, 0),
                (here.sib, 1, 1, here.sib, 1),
                (here.y_same, 0, 2, here.y_same, 0),
                (here.x_same, 1, 2, here.x_same, 1),
                (here.y_other, 0, 3, here.y_other, 0),
                (here.x_other, 1, 3, here.x_other, 1),
            )
        ):
            send = push(
                rows_of(owner, half),
                slot(number, k),
                held_send.at[unit, count],
                held_recv.at[unit, number, k],
                z,
                goal,
            )
            send.start()
            at_end.append((None, [send]))

    def put_together(index, number):
        part, plane = units[index]
        unit = unit_of(part, plane)
        owner, _, experts = targets[number]
        for k in range(4):
            wait_for(
                held.at[unit, number, pl.ds(k * capacity, capacity)],
                held_recv.at[unit, number, k],
            )
        select = one_hot(pos_ref, experts, plane * PLANE + owner, capacity)
        return lax.dot_general(
            select,
            held[unit, number],
            (((0,), (0,)), ((), ())),
            preferred_element_type=jnp.float32,
        )

    def first(index):
        part, plane = units[index]
        unit = unit_of(part, plane)
        slot = index % 4
        for half in range(2):
            send = push(
                dense_out.at[half, slot],
                dense_in.at[half, unit],
                dense_send.at[half, slot],
                dense_recv.at[half, unit],
                z,
                (here.x_same, here.y_same)[half],
            )
            if index >= 4:
                send.wait_send()
            dense_out[half, slot] = put_together(index, 2 + half).astype(jnp.bfloat16)
            send.start()
            if index >= len(units) - 4:
                at_end.append((None, [send]))

    def hand_on(index, plane_here, up):
        part, plane = units[index]
        unit = unit_of(part, plane)
        goal = plane_here + 1 if up else plane_here - 1
        slot = unit if up or goal != plane else CUTS * LINE + part
        send = push(
            sums.at[unit], passed.at[slot], pass_send.at[unit], pass_recv.at[slot], goal, e
        )
        send.start()
        return send

    def second(index):
        part, plane = units[index]
        unit = unit_of(part, plane)
        for half in range(2):
            wait_for(dense_in.at[half, unit], dense_recv.at[half, unit])
            whole = put_together(index, half) + dense_in[half, unit].astype(jnp.float32)
            sums[unit, :, half * CUT : (half + 1) * CUT] = whole.astype(jnp.bfloat16)
        if plane > 0:

            @pl.when(z == 0)
            def _():
                hand_on(index, 0, True)

        if plane < LINE - 1:

            @pl.when(z == LINE - 1)
            def _():
                hand_on(index, LINE - 1, False)

    def third(index, hop):
        part, plane = units[index]
        unit = unit_of(part, plane)
        ways = []
        if hop < plane and hop < LINE - 1:
            ways.append((hop, True))
        if LINE - 1 - hop > plane and LINE - 1 - hop > 0:
            ways.append((LINE - 1 - hop, False))
        for plane_here, up in ways:

            @pl.when(z == plane_here)
            def _():
                wait_for(passed.at[unit], pass_recv.at[unit])
                total = sums[unit].astype(jnp.float32) + passed[unit].astype(jnp.float32)
                sums[unit] = total.astype(jnp.bfloat16)
                hand_on(index, plane_here, up)

    own = pl.ds(e, 1)
    gates_plane[:, own] = gate_grad_ref[:, own]
    gate_moves = in_plane_of(here, gate_grad_ref, gates_plane, gate_plane_send, gate_plane_recv)
    gate_moves_on = along_line(here, gates_plane, gate_out_ref, gate_line_send, gate_line_recv)
    for move in gate_moves:
        move.start()

    count = len(units)
    for ahead in range(AHEAD):
        compact(ahead)
    for step in range(count + 3):
        if step + AHEAD < count:
            compact(step + AHEAD)
        if step == 2:
            for owner in here.plane:
                wait_for(gates_plane.at[:, owner], gate_plane_recv.at[owner])
            gate_out_ref[z] = gates_plane[z]
            for move in gate_moves_on:
                move.start()
        if step < count:
            first(step)
        if 0 <= step - 1 < count:
            second(step - 1)
        for hop in (1, 2):
            if 0 <= step - 1 - hop < count:
                third(step - 1 - hop, hop)

    for plane in here.line:
        wait_for(gate_out_ref.at[plane], gate_line_recv.at[plane])
    for move in gate_moves + gate_moves_on:
        move.wait_send()
    for part in range(CUTS):
        unit = part * LINE + z
        for half in range(2):
            out_ref[:, cut_columns(half, part)] = sums[
                unit, :, half * CUT : (half + 1) * CUT
            ].astype(jnp.float32)
        for going, slot in ((z > 0, unit), (z < LINE - 1, CUTS * LINE + part)):

            @pl.when(going)
            def _():
                wait_for(passed.at[slot], pass_recv.at[slot])
                for half in range(2):
                    columns = cut_columns(half, part)
                    out_ref[:, columns] = out_ref[:, columns] + passed[
                        slot, :, half * CUT : (half + 1) * CUT
                    ].astype(jnp.float32)

    for _, sends in at_end:
        for send in sends:
            send.wait_send()
    for part, plane in units:
        unit = unit_of(part, plane)

        @pl.when(z != plane)
        def _():
            push(
                sums.at[unit], passed.at[unit], pass_send.at[unit], pass_recv.at[unit], z, here.sib
            ).wait_send()


def combine(rows, positions, gate_grad, collective_id):
    capacity = rows.shape[1]
    bf16 = jnp.bfloat16
    dma = pltpu.SemaphoreType.DMA
    units = CUTS * LINE
    return pl.pallas_call(
        combine_kernel,
        out_shape=[
            jax.ShapeDtypeStruct((DEVICE_TOKENS, MODEL_WIDTH), jnp.float32),
            jax.ShapeDtypeStruct(GATE_SHAPE, jnp.float32),
        ],
        in_specs=[
            pl.BlockSpec(memory_space=pltpu.VMEM),
            pl.BlockSpec(memory_space=pltpu.VMEM),
            pl.BlockSpec(memory_space=pl.ANY),
        ],
        out_specs=[pl.BlockSpec(memory_space=pltpu.VMEM)] * 2,
        scratch_shapes=[
            pltpu.VMEM(GATE_SHAPE, jnp.float32),
            pltpu.VMEM((units, 4, 4 * capacity, CUT), bf16),
            pltpu.VMEM((2, 4, DEVICE_TOKENS, CUT), bf16),
            pltpu.VMEM((2, units, DEVICE_TOKENS, CUT), bf16),
            pltpu.VMEM((units, DEVICE_TOKENS, 2 * CUT), bf16),
            pltpu.VMEM((units + CUTS, DEVICE_TOKENS, 2 * CUT), bf16),
            dma((units, 12)),
            dma((units, 4, 4)),
            dma((2, 4)),
            dma((2, units)),
            dma((units,)),
            dma((units + CUTS,)),
            dma((PLANE,)),
            dma((PLANE,)),
            dma((LINE,)),
            dma((LINE,)),
        ],
        compiler_params=pltpu.CompilerParams(
            collective_id=collective_id, has_side_effects=True, vmem_limit_bytes=60 * 2**20
        ),
    )(positions, gate_grad, rows)


def near_first(z):
    power_of_four = (
        1 + 3 * z + lax.div(z * (z - 1), 2) * 9 + lax.div(z * (z - 1) * (z - 2), 6) * 27
    )
    orders = ((0, 1, 2, 3), (1, 0, 2, 3), (2, 3, 1, 0), (3, 2, 1, 0))
    tables = [
        sum(order[step] * 4**plane for plane, order in enumerate(orders)) for step in range(LINE)
    ]
    return [lax.rem(lax.div(jnp.int32(table), power_of_four), 4) for table in tables]


def wait_for(buffer, sem):
    pltpu.make_async_copy(buffer, buffer, sem).wait()


def spread_in_plane(here, whole, rows, halves, plane, recv, send, number, at_end, mine):
    z = here.z

    def piece(owner, half):
        start, size = halves[half]
        return whole.at[pl.ds((plane * PLANE + owner) * rows + start, size)]

    def to(owner, half, goal, count):
        copy = push(
            piece(owner, half),
            piece(owner, half),
            send.at[number, count],
            recv.at[plane * PLANE + owner, half],
            z,
            goal,
        )
        copy.start()
        at_end.append((None, [copy]))

    def arrived(owner, half):
        wait_for(piece(owner, half), recv.at[plane * PLANE + owner, half])

    ways = range(len(halves))

    def first():
        for half in ways:
            mine(half)
            to(here.e, half, here.x_same, 3 * half)
            to(here.e, half, here.y_same, 3 * half + 1)
            to(here.e, half, here.sib, 3 * half + 2)

    def second():
        for half in ways:
            arrived(here.x_same, half)
            if half == len(halves) - 1:
                to(here.x_same, half, here.y_same, 6)
            to(here.x_same, half, here.sib, 7 + half)
            arrived(here.y_same, half)
            if half == 0 and len(halves) > 1:
                to(here.y_same, half, here.x_same, 9)
            to(here.y_same, half, here.sib, 10 + half)

    def third():
        for half in ways:
            arrived(here.d_same, half)
            to(here.d_same, half, here.sib, 12 + half)

    def last():
        for owner in (here.sib, here.x_other, here.y_other, here.d_other):
            for half in ways:
                arrived(owner, half)

    return first, second, third, last


def finish(at_end):
    for go, sends in at_end:
        if go is None:
            for send in sends:
                send.wait_send()
        else:

            @pl.when(go)
            def _():
                for send in sends:
                    send.wait_send()


def halves_of(rows):
    return ((0, rows // 2), (rows // 2, rows // 2)) if rows >= 32 else ((0, rows),)


def gather_kernel(kinds, *refs):
    total = len(kinds)
    sources, wholes, scratch = refs[:total], refs[total : 2 * total], refs[2 * total :]
    here = Place()
    z, e = here.z, here.e
    here.greet()
    planes = near_first(z)
    at_end = []
    locals_ = []
    steps = [[] for _ in range(LINE)]
    arrays = []
    for index, (source, whole) in enumerate(zip(sources, wholes)):
        recv, send, line_send, own = scratch[4 * index : 4 * index + 4]
        passing = scratch[4 * total + index]
        kind = kinds[index]
        rows = source.shape[0] // (PLANE if kind == "weight" else 1)
        halves = halves_of(rows)
        arrays.append((kind, source, whole, rows, halves, recv, send, line_send))
        if kind == "block":
            base = (z * PLANE + e) * rows
        else:
            base = z * source.shape[0]
        first = pltpu.make_async_copy(source, passing, own.at[0])
        first.start()
        goal = whole.at[pl.ds(base, source.shape[0])]
        locals_.append((kind, first, pltpu.make_async_copy(passing, goal, own.at[1])))

    def line_piece(array, plane, half):
        kind, _, whole, rows, halves, _, _, _ = array
        start, size = halves[half]
        owner = plane if kind in ("plane", "late") else plane * PLANE + e
        return whole.at[pl.ds(owner * rows + start, size)]

    def line_sem(array, plane, half):
        owner = plane if array[0] in ("plane", "late") else plane * PLANE + e
        return array[5].at[owner, half]

    def along(array, step, half):
        plane = planes[step]
        kind, source, _, rows, halves, _, _, line_send = array
        for direction in range(2):
            if direction == 0:
                go = (plane <= z) & (z < LINE - 1)
                goal = z + 1
            else:
                go = (plane >= z) & (z > 0)
                goal = z - 1
            if step == 0:
                start, size = halves[half]
                offset = e * rows + start if kind == "weight" else start
                origin = source.at[pl.ds(offset, size)]
            else:
                origin = line_piece(array, plane, half)
            copy = push(
                origin,
                line_piece(array, plane, half),
                line_send.at[step, half, direction],
                line_sem(array, plane, half),
                goal,
                e,
            )

            @pl.when(go)
            def _():
                copy.start()

            at_end.append((go, [copy]))

    for array in arrays:
        if array[0] != "late":
            for half in range(len(array[4])):
                along(array, 0, half)
    for _, first, second in locals_:
        first.wait()
        second.start()
    for kind, _, second in locals_:
        if kind == "block":
            second.wait()

    later = []

    def arrive(step):
        work = []
        for array in arrays:
            kind, _, whole, rows, halves, recv, send, _ = array

            def mine(half, array=array):
                if step > 0:
                    wait_for(
                        line_piece(array, planes[step], half),
                        line_sem(array, planes[step], half),
                    )
                    along(array, step, half)

            if kind == "late":
                continue
            if kind == "plane" or (kind == "weight" and step == 0):
                if step > 0:
                    for half in range(len(halves)):
                        mine(half)
                continue
            first, second, third, last = spread_in_plane(
                here, whole, rows, halves, planes[step], recv, send, step, at_end, mine
            )
            first()
            work.append((second, third, last))
        later.append(work)

    def arrive_late(step):
        for array in arrays:
            if array[0] == "late":
                for half in range(len(array[4])):
                    if step > 0:
                        wait_for(
                            line_piece(array, planes[step], half),
                            line_sem(array, planes[step], half),
                        )
                    along(array, step, half)

    for step in range(LINE + 2):
        if step < LINE:
            arrive(step)
        if step >= 2:
            arrive_late(step - 2)
        if 0 <= step - 1 < LINE:
            for second, _, _ in later[step - 1]:
                second()
        if 0 <= step - 2 < LINE:
            for _, third, _ in later[step - 2]:
                third()
    for work in later:
        for _, _, last in work:
            last()
    for kind, _, second in locals_:
        if kind != "block":
            second.wait()
    finish(at_end)


def gather_all(weights, line, late, block, collective_id):
    sources = tuple(weights) + (line, late, block)
    kinds = ("weight",) * len(weights) + ("plane", "late", "block")
    parts = [LINE] * (len(sources) - 1) + [LINE * PLANE]
    dma = pltpu.SemaphoreType.DMA
    scratch = []
    for _ in sources:
        scratch += [dma((LINE * PLANE, 2)), dma((LINE, 16)), dma((LINE, 2, 2)), dma((2,))]
    scratch += [pltpu.VMEM(array.shape, array.dtype) for array in sources]
    return pl.pallas_call(
        functools.partial(gather_kernel, kinds),
        out_shape=[
            jax.ShapeDtypeStruct((array.shape[0] * part,) + array.shape[1:], array.dtype)
            for array, part in zip(sources, parts)
        ],
        in_specs=[pl.BlockSpec(memory_space=pl.ANY)] * len(sources),
        out_specs=[pl.BlockSpec(memory_space=pl.ANY)] * len(sources),
        scratch_shapes=scratch,
        compiler_params=pltpu.CompilerParams(
            collective_id=collective_id, has_side_effects=True, vmem_limit_bytes=32 * 2**20
        ),
    )(*sources)


def add_into(goal, *terms):
    rows, columns = goal.shape

    def some(index, carry):
        at = pl.ds(pl.multiple_of(index * 16, 16), 16)
        for start in range(0, columns, 1024):
            cut = slice(start, start + 1024)
            total = goal[at, cut].astype(jnp.float32)
            for term in terms:
                total = total + term[at, cut].astype(jnp.float32)
            goal[at, cut] = total.astype(goal.dtype)
        return carry

    lax.fori_loop(0, rows // 16, some, 0)


def reduce_kernel(count, *refs):
    sources, wholes, scratch = refs[:count], refs[count : 2 * count], refs[2 * count :]
    here = Place()
    z, e = here.z, here.e
    here.greet()
    at_end = []
    owners = (here.d_same, here.x_same, here.y_same, here.e)
    other_owners = (here.d_other, here.x_other, here.y_other, here.sib)
    units = [(plane, index) for index in range(count) for plane in FAR_FIRST]
    names = (
        "held", "sib", "half", "side", "passed",
        "held_recv", "sib_recv", "sib_send", "half_recv", "half_send",
        "side_recv", "side_send", "pass_recv", "pass_send", "own", "out_recv", "out_send",
    )
    per = len(names)
    buffers = [dict(zip(names, scratch[per * i : per * i + per])) for i in range(count)]
    rows_of = [source.shape[0] // (LINE * PLANE) for source in sources]

    def sent(copy):
        copy.start()
        at_end.append((None, [copy]))

    def load(number):
        plane, index = units[number]
        b, rows, source = buffers[index], rows_of[index], sources[index]
        for kind in range(4):
            mine = source.at[pl.ds((plane * PLANE + owners[kind]) * rows, rows)]
            theirs = source.at[pl.ds((plane * PLANE + other_owners[kind]) * rows, rows)]
            sent(
                push(
                    theirs,
                    b["sib"].at[plane, kind],
                    b["sib_send"].at[plane, kind],
                    b["sib_recv"].at[plane, kind],
                    z,
                    here.sib,
                )
            )
            pltpu.make_async_copy(
                mine, b["held"].at[plane, kind], b["held_recv"].at[plane, kind]
            ).start()

    def both(number, kind):
        plane, index = units[number]
        b = buffers[index]
        wait_for(b["held"].at[plane, kind], b["held_recv"].at[plane, kind])
        wait_for(b["sib"].at[plane, kind], b["sib_recv"].at[plane, kind])
        add_into(b["held"].at[plane, kind], b["sib"].at[plane, kind])

    def first(number):
        plane, index = units[number]
        b, rows = buffers[index], rows_of[index]
        both(number, 0)
        for half, goal in enumerate((here.y_same, here.x_same)):
            at = pl.ds(half * rows // 2, rows // 2)
            sent(
                push(
                    b["held"].at[plane, 0, at],
                    b["half"].at[plane, at],
                    b["half_send"].at[plane, half],
                    b["half_recv"].at[plane, half],
                    z,
                    goal,
                )
            )
        both(number, 1)
        both(number, 2)

    def second(number):
        plane, index = units[number]
        b, rows = buffers[index], rows_of[index]
        for half, goal in enumerate((here.x_same, here.y_same)):
            at = pl.ds(half * rows // 2, rows // 2)
            wait_for(b["half"].at[plane, at], b["half_recv"].at[plane, half])
            add_into(b["held"].at[plane, 1 + half, at], b["half"].at[plane, at])
            sent(
                push(
                    b["held"].at[plane, 1 + half],
                    b["side"].at[half, plane],
                    b["side_send"].at[half, plane],
                    b["side_recv"].at[half, plane],
                    z,
                    goal,
                )
            )
        both(number, 3)

    def hand_on(number, plane_here, up):
        plane, index = units[number]
        b = buffers[index]
        goal = plane_here + 1 if up else plane_here - 1
        slot = plane if up or goal != plane else LINE
        push(
            b["held"].at[plane, 3],
            b["passed"].at[slot],
            b["pass_send"].at[plane],
            b["pass_recv"].at[slot],
            goal,
            e,
        ).start()

    def third(number):
        plane, index = units[number]
        b = buffers[index]
        for half in range(2):
            wait_for(b["side"].at[half, plane], b["side_recv"].at[half, plane])
        add_into(b["held"].at[plane, 3], b["side"].at[0, plane], b["side"].at[1, plane])
        if plane > 0:

            @pl.when(z == 0)
            def _():
                hand_on(number, 0, True)

        if plane < LINE - 1:

            @pl.when(z == LINE - 1)
            def _():
                hand_on(number, LINE - 1, False)

    def hop(number, distance):
        plane, index = units[number]
        b = buffers[index]
        ways = []
        if distance < plane and distance < LINE - 1:
            ways.append((distance, True))
        if LINE - 1 - distance > plane and LINE - 1 - distance > 0:
            ways.append((LINE - 1 - distance, False))
        for plane_here, up in ways:

            @pl.when(z == plane_here)
            def _():
                wait_for(b["passed"].at[plane], b["pass_recv"].at[plane])
                add_into(b["held"].at[plane, 3], b["passed"].at[plane])
                hand_on(number, plane_here, up)

    def spread(index):
        b, rows, whole = buffers[index], rows_of[index], wholes[index]
        for going, slot in ((z > 0, z), (z < LINE - 1, LINE)):

            @pl.when(going)
            def _():
                wait_for(b["passed"].at[slot], b["pass_recv"].at[slot])
                add_into(b["held"].at[z, 3], b["passed"].at[slot])

        copy = pltpu.make_async_copy(
            b["held"].at[z, 3], whole.at[pl.ds(e * rows, rows)], b["own"].at[0]
        )
        copy.start()
        copy.wait()
        return spread_in_plane(
            here,
            whole,
            rows,
            halves_of(rows),
            0,
            b["out_recv"],
            b["out_send"],
            0,
            at_end,
            lambda half: None,
        )

    steps = len(units)
    ready = LINE - 1 + 2 + 3
    spreads = {}
    load(0)
    load(1)
    for step in range((count - 1) * LINE + ready + 3):
        if step + 2 < steps:
            load(step + 2)
        if step < steps:
            first(step)
        if 0 <= step - 1 < steps:
            second(step - 1)
        if 0 <= step - 2 < steps:
            third(step - 2)
        for distance in (1, 2):
            if 0 <= step - 2 - distance < steps:
                hop(step - 2 - distance, distance)
        for index in range(count):
            stage = step - index * LINE - ready
            if stage == 0:
                spreads[index] = spread(index)
            if 0 <= stage < 3:
                spreads[index][stage]()
    for index in range(count):
        spreads[index][3]()
    finish(at_end)
    for plane, index in units:
        b = buffers[index]

        @pl.when(z != plane)
        def _():
            push(
                b["held"].at[plane, 3],
                b["passed"].at[plane],
                b["pass_send"].at[plane],
                b["pass_recv"].at[plane],
                z,
                here.sib,
            ).wait_send()


def reduce_all(arrays, collective_id):
    dma = pltpu.SemaphoreType.DMA
    scratch = []
    for array in arrays:
        rows = array.shape[0] // (LINE * PLANE)
        block = (rows, array.shape[1])
        scratch += [
            pltpu.VMEM((LINE, 4) + block, array.dtype),
            pltpu.VMEM((LINE, 4) + block, array.dtype),
            pltpu.VMEM((LINE,) + block, array.dtype),
            pltpu.VMEM((2, LINE) + block, array.dtype),
            pltpu.VMEM((LINE + 1,) + block, array.dtype),
            dma((LINE, 4)),
            dma((LINE, 4)),
            dma((LINE, 4)),
            dma((LINE, 2)),
            dma((LINE, 2)),
            dma((2, LINE)),
            dma((2, LINE)),
            dma((LINE + 1,)),
            dma((LINE,)),
            dma((1,)),
            dma((PLANE, 2)),
            dma((1, 16)),
        ]
    return pl.pallas_call(
        functools.partial(reduce_kernel, len(arrays)),
        out_shape=[
            jax.ShapeDtypeStruct((array.shape[0] // LINE, array.shape[1]), array.dtype)
            for array in arrays
        ],
        in_specs=[pl.BlockSpec(memory_space=pl.ANY)] * len(arrays),
        out_specs=[pl.BlockSpec(memory_space=pl.ANY)] * len(arrays),
        scratch_shapes=scratch,
        compiler_params=pltpu.CompilerParams(
            collective_id=collective_id, has_side_effects=True, vmem_limit_bytes=60 * 2**20
        ),
    )(*arrays)


ROWS = 256
FORWARD_ROWS = 256
LOG2_E = 1.4426950408889634
GROUP = QUERY_HEADS // KEY_VALUE_HEADS
SCORE_SCALE = HEAD_SIZE ** (-0.5)


def across(left, right, contract):
    return lax.dot_general(
        left, right, ((contract[:1], contract[1:]), ((), ())), preferred_element_type=jnp.float32
    )


def head_norm(raw, gain):
    scale = lax.rsqrt(jnp.mean(raw * raw, axis=-1, keepdims=True) + EPSILON)
    unit = raw * scale
    return scale, unit, unit * gain


def turned(rows, sine):
    return pltpu.roll(rows, HEAD_SIZE // 2, 1) * sine


def masked(segment_column, segment_row):
    shape = (segment_column.shape[0], segment_row.shape[1])
    before = lax.broadcasted_iota(jnp.int32, shape, 1) <= lax.broadcasted_iota(jnp.int32, shape, 0)
    return jnp.where(before & (segment_column == segment_row), 0.0, -1e30)


def row_blocks(length, rows=ROWS):
    return [(start, start + rows) for start in range(0, length, rows)]


def attention_kernel(
    query_ref,
    key_ref,
    value_ref,
    cosine_ref,
    sine_ref,
    query_gain_ref,
    key_gain_ref,
    column_ref,
    row_ref,
    mixed_ref,
    query_rot_ref,
    key_rot_ref,
    value_low_ref,
    total_ref,
    bias,
):
    low = jnp.bfloat16
    length = bias.shape[0]

    @pl.when(pl.program_id(0) == 0)
    def _():
        bias[...] = masked(column_ref[...], row_ref[...])

    cosine, sine = cosine_ref[...], sine_ref[...]
    _, _, key = head_norm(key_ref[...], key_gain_ref[...])
    key_rot = (key * cosine + turned(key, sine)).astype(low)
    key_rot_ref[...] = key_rot
    value = value_ref[...].astype(low)
    value_low_ref[...] = value
    totals = []
    for head in range(GROUP):
        columns = slice(head * HEAD_SIZE, (head + 1) * HEAD_SIZE)
        _, _, query = head_norm(query_ref[:, columns], query_gain_ref[...])
        query_rot = (query * cosine + turned(query, sine)).astype(low)
        query_rot_ref[:, columns] = query_rot
        parts = []
        for start, end in row_blocks(length, FORWARD_ROWS):
            scores = across(query_rot[start:end], key_rot[:end], (1, 1)) + bias[start:end, :end]
            peak = jnp.max(scores, axis=-1, keepdims=True)
            weights = jnp.exp2((scores - peak) * (SCORE_SCALE * LOG2_E))
            total = jnp.sum(weights, axis=-1, keepdims=True)
            mixed = across(weights.astype(low), value[:end], (1, 0)) * (1.0 / total)
            mixed_ref[start:end, columns] = mixed.astype(low)
            parts.append(peak * SCORE_SCALE + jnp.log(total))
        totals.append(jnp.concatenate(parts, axis=0))
    total_ref[0] = jnp.concatenate(totals, axis=1)


def attention(qkv, segments, cosine, sine, query_gain, key_gain):
    length = qkv.shape[0]
    width = GROUP * HEAD_SIZE
    low = jnp.bfloat16
    whole = lambda *shape: pl.BlockSpec(shape, lambda j: (0,) * len(shape))
    heads = lambda first: pl.BlockSpec((length, HEAD_SIZE), lambda j: (0, first + j))
    key_start = QUERY_HEADS
    return pl.pallas_call(
        attention_kernel,
        grid=(KEY_VALUE_HEADS,),
        in_specs=[
            pl.BlockSpec((length, width), lambda j: (0, j)),
            heads(key_start),
            heads(key_start + KEY_VALUE_HEADS),
            whole(length, HEAD_SIZE),
            whole(length, HEAD_SIZE),
            whole(1, HEAD_SIZE),
            whole(1, HEAD_SIZE),
            whole(length, 1),
            whole(1, length),
        ],
        out_specs=[
            pl.BlockSpec((length, width), lambda j: (0, j)),
            pl.BlockSpec((length, width), lambda j: (0, j)),
            heads(0),
            heads(0),
            pl.BlockSpec((1, length, GROUP), lambda j: (j, 0, 0)),
        ],
        out_shape=[
            jax.ShapeDtypeStruct((length, QUERY_HEADS * HEAD_SIZE), low),
            jax.ShapeDtypeStruct((length, QUERY_HEADS * HEAD_SIZE), low),
            jax.ShapeDtypeStruct((length, KEY_VALUE_HEADS * HEAD_SIZE), low),
            jax.ShapeDtypeStruct((length, KEY_VALUE_HEADS * HEAD_SIZE), low),
            jax.ShapeDtypeStruct((KEY_VALUE_HEADS, length, GROUP), jnp.float32),
        ],
        scratch_shapes=[pltpu.VMEM((length, length), jnp.float32)],
        compiler_params=pltpu.CompilerParams(vmem_limit_bytes=48 * 2**20),
    )(qkv, qkv, qkv, cosine, sine, query_gain, key_gain, segments.T, segments)


def attention_back_kernel(
    query_ref,
    key_ref,
    query_rot_ref,
    key_rot_ref,
    value_ref,
    mixed_grad_ref,
    total_ref,
    cosine_ref,
    sine_ref,
    query_gain_ref,
    key_gain_ref,
    column_ref,
    row_ref,
    query_out_ref,
    key_out_ref,
    value_out_ref,
    gains_ref,
    bias,
):
    low = jnp.bfloat16
    length = bias.shape[0]

    @pl.when(pl.program_id(0) == 0)
    def _():
        bias[...] = masked(column_ref[...], row_ref[...])
        gains_ref[...] = jnp.zeros_like(gains_ref)

    cosine, sine = cosine_ref[...], sine_ref[...]
    key_rot, value = key_rot_ref[...], value_ref[...]

    def before_norm(grad_rot, raw, gain):
        grad = grad_rot * cosine - turned(grad_rot, sine)
        scale, unit, _ = head_norm(raw, gain)
        gain_grad = jnp.sum(grad * unit, axis=0, keepdims=True)
        pulled = grad * gain
        back = scale * (pulled - unit * jnp.mean(pulled * unit, axis=-1, keepdims=True))
        return back.astype(low), gain_grad

    blocks = row_blocks(length)
    key_grads = [jnp.zeros((ROWS, HEAD_SIZE), jnp.float32) for _ in blocks]
    value_grads = [jnp.zeros((ROWS, HEAD_SIZE), jnp.float32) for _ in blocks]
    query_gain_grad = jnp.zeros((1, HEAD_SIZE), jnp.float32)
    for head in range(GROUP):
        columns = slice(head * HEAD_SIZE, (head + 1) * HEAD_SIZE)
        query_rot = query_rot_ref[:, columns]
        mixed_grad = mixed_grad_ref[:, columns]
        total = total_ref[0, :, head : head + 1]
        parts = []
        for start, end in blocks:
            scores = across(query_rot[start:end], key_rot[:end], (1, 1)) * SCORE_SCALE
            probs = jnp.exp(scores + bias[start:end, :end] - total[start:end])
            prob_grad = across(mixed_grad[start:end], value[:end], (1, 1))
            weighted = prob_grad * probs
            row_sum = jnp.sum(weighted, axis=-1, keepdims=True)
            score_low = (weighted - probs * row_sum).astype(low)
            probs_low = probs.astype(low)
            parts.append(across(score_low, key_rot[:end], (1, 0)) * SCORE_SCALE)
            key_part = across(score_low, query_rot[start:end], (0, 0))
            value_part = across(probs_low, mixed_grad[start:end], (0, 0))
            for index, (first, last) in enumerate(blocks):
                if last <= end:
                    key_grads[index] = key_grads[index] + key_part[first:last]
                    value_grads[index] = value_grads[index] + value_part[first:last]
        back, gain_grad = before_norm(
            jnp.concatenate(parts, axis=0), query_ref[:, columns], query_gain_ref[...]
        )
        query_out_ref[:, columns] = back
        query_gain_grad = query_gain_grad + gain_grad
    back, key_gain_grad = before_norm(
        jnp.concatenate(key_grads, axis=0) * SCORE_SCALE, key_ref[...], key_gain_ref[...]
    )
    key_out_ref[...] = back
    value_out_ref[...] = jnp.concatenate(value_grads, axis=0).astype(low)
    gains_ref[0:1] += query_gain_grad
    gains_ref[1:2] += key_gain_grad


def attention_back(
    qkv, query_rot, key_rot, value, mixed_grad, totals, segments, cosine, sine, query_gain, key_gain
):
    length = qkv.shape[0]
    width = GROUP * HEAD_SIZE
    low = jnp.bfloat16
    whole = lambda *shape: pl.BlockSpec(shape, lambda j: (0,) * len(shape))
    heads = lambda first: pl.BlockSpec((length, HEAD_SIZE), lambda j: (0, first + j))
    wide = pl.BlockSpec((length, width), lambda j: (0, j))
    return pl.pallas_call(
        attention_back_kernel,
        grid=(KEY_VALUE_HEADS,),
        in_specs=[
            wide,
            heads(QUERY_HEADS),
            wide,
            heads(0),
            heads(0),
            wide,
            pl.BlockSpec((1, length, GROUP), lambda j: (j, 0, 0)),
            whole(length, HEAD_SIZE),
            whole(length, HEAD_SIZE),
            whole(1, HEAD_SIZE),
            whole(1, HEAD_SIZE),
            whole(length, 1),
            whole(1, length),
        ],
        out_specs=[wide, heads(0), heads(0), whole(8, HEAD_SIZE)],
        out_shape=[
            jax.ShapeDtypeStruct((length, QUERY_HEADS * HEAD_SIZE), low),
            jax.ShapeDtypeStruct((length, KEY_VALUE_HEADS * HEAD_SIZE), low),
            jax.ShapeDtypeStruct((length, KEY_VALUE_HEADS * HEAD_SIZE), low),
            jax.ShapeDtypeStruct((8, HEAD_SIZE), jnp.float32),
        ],
        scratch_shapes=[pltpu.VMEM((length, length), jnp.float32)],
        compiler_params=pltpu.CompilerParams(vmem_limit_bytes=56 * 2**20),
    )(
        qkv,
        qkv,
        query_rot,
        key_rot,
        value,
        mixed_grad,
        totals,
        cosine,
        sine,
        query_gain,
        key_gain,
        segments.T,
        segments,
    )


UNITS = 16
GATE_SHAPE = (LINE, PLANE, 1, DEVICE_TOKENS)
LAG = 4
CHUNK = 2


def expert_kernel(
    pos_ref,
    gates_ref,
    w_gate_ref,
    w_up_ref,
    w_down_ref,
    routed_ref,
    cotangent_ref,
    early_line_ref,
    early_x_ref,
    early_y_ref,
    routed_rows_ref,
    cotangent_rows_ref,
    out_ref,
    out_second_ref,
    back_ref,
    act_ref,
    gate_low_ref,
    up_low_ref,
    gate_grad_ref,
    line,
    dense,
    own_held,
    near,
    side,
    gates_line,
    gates_here,
    picked,
    taken,
    out_held,
    back_held,
    act_held,
    gate_held,
    up_held,
    line_send,
    line_recv,
    dense_send,
    dense_recv,
    side_send,
    row_send,
    row_recv,
    own_sem,
    near_sem,
    side_sem,
    taken_sem,
    put_sem,
    gate_line_send,
    gate_line_recv,
    gate_plane_send,
    gate_plane_recv,
):
    here = Place()
    z, e = here.z, here.e
    capacity = out_ref.shape[1]
    low, f32 = jnp.bfloat16, jnp.float32
    rows_refs = (routed_rows_ref, cotangent_rows_ref)
    here.greet()
    targets = target_sets(here)
    planes = near_first(z)
    packed = planes[0] + 4 * planes[1] + 16 * planes[2] + 64 * planes[3]
    inputs = (routed_ref, cotangent_ref)

    def plane_of(step):
        power = (
            1
            + 3 * step
            + lax.div(step * (step - 1), 2) * 9
            + lax.div(step * (step - 1) * (step - 2), 6) * 27
        )
        return lax.rem(lax.div(packed, power), 4)

    def unit(i):
        return plane_of(lax.div(i, 4)), lax.rem(lax.div(i, 2), 2), lax.rem(i, 2)

    def columns(half, part):
        return pl.ds(pl.multiple_of(half * 2 * PART + part * PART, PART), PART)

    firsts = [
        pltpu.make_async_copy(inputs[stream], own_held.at[stream], near_sem.at[stream])
        for stream in range(2)
    ]
    for first in firsts:
        first.start()
    for stream in range(2):
        firsts[stream].wait()
        for part in range(stream, 2):
            for half in range(2):
                pltpu.make_async_copy(
                    own_held.at[stream, :, part_columns(half, part)],
                    line.at[stream, part, z, half],
                    line_recv.at[stream, part, z, half],
                ).start()
    at_an_end = (z == 0) | (z == LINE - 1)
    gates_line[z] = gates_ref[z]
    gate_moves = along_line(here, gates_ref, gates_line, gate_line_send, gate_line_recv)
    gate_moves_on = in_plane_of(here, gates_line, gates_here, gate_plane_send, gate_plane_recv)
    for move in gate_moves:
        move.start()

    def spread_gates():
        for plane in here.line:
            wait_for(gates_line.at[plane], gate_line_recv.at[plane])
        own = pl.ds(e, 1)
        gates_here[:, own] = gates_line[:, own]
        for move in gate_moves_on:
            move.start()

    def wait_gates():
        for owner in here.plane:
            wait_for(gates_here.at[:, owner], gate_plane_recv.at[owner])

    def forwards(i):
        plane, stream, part = unit(i)
        out = []
        for half in range(2):
            for direction in range(2):
                goal = z + 1 - 2 * direction
                out.append(
                    push(
                        line.at[stream, part, plane, half],
                        line.at[stream, part, plane, half],
                        line_send.at[i, half, direction],
                        line_recv.at[stream, part, plane, half],
                        goal,
                        e,
                    )
                )
        return out

    def side_forwards(i):
        plane, stream, part = unit(i)
        return [
            push(
                dense.at[stream, part, plane, half],
                dense.at[stream, part, plane, half],
                side_send.at[lax.div(i, 4), half, direction],
                dense_recv.at[stream, part, plane, half],
                z + 1 - 2 * direction,
                e,
            )
            for half in range(2)
            for direction in range(2)
        ]

    def along(i, sends, act):
        plane = unit(i)[0]

        @pl.when((plane <= z) & (z < LINE - 1))
        def _():
            act(sends[0])
            act(sends[2])

        @pl.when((plane >= z) & (z > 0))
        def _():
            act(sends[1])
            act(sends[3])

    def side_first(i):
        return lax.rem(i, 4) == 3

    def early(i):
        return lax.rem(i, 4) == 2

    def denses(i):
        plane, stream, part = unit(i)
        return [
            push(
                line.at[stream, part, plane, half],
                dense.at[stream, part, plane, half],
                dense_send.at[i, half],
                dense_recv.at[stream, part, plane, half],
                z,
                (here.x_same, here.y_same)[half],
            )
            for half in range(2)
        ]

    def pass_on(i):
        plane, stream, part = unit(i)
        for half in range(2):
            wait_for(line.at[stream, part, plane, half], line_recv.at[stream, part, plane, half])
        along(i, forwards(i), lambda send: send.start())

    def pass_side_on(i):
        plane, stream, part = unit(i)
        for half in range(2):
            wait_for(dense.at[stream, part, plane, half], dense_recv.at[stream, part, plane, half])
        along(i, side_forwards(i), lambda send: send.start())

    def arrive(i):
        plane, stream, part = unit(i)

        @pl.when(early(i))
        def _():
            for half in range(2):
                pltpu.make_async_copy(
                    early_line_ref.at[plane, :, pl.ds(half * PART, PART)],
                    near.at[half],
                    near_sem.at[half],
                ).start()

        @pl.when(jnp.logical_not(early(i)))
        def _():
            @pl.when((i >= 4) & at_an_end)
            def _():
                for half in range(2):
                    wait_for(
                        line.at[stream, part, plane, half], line_recv.at[stream, part, plane, half]
                    )

            for half in range(2):
                pltpu.make_async_copy(
                    line.at[stream, part, plane, half], near.at[half], near_sem.at[half]
                ).start()

            @pl.when(jnp.logical_not(side_first(i)))
            def _():
                for send in denses(i):
                    send.start()

    def arrive_side(i):
        plane, stream, part = unit(i)

        @pl.when(early(i))
        def _():
            for half, source in enumerate((early_x_ref, early_y_ref)):
                pltpu.make_async_copy(source.at[plane], side.at[half], side_sem.at[half]).start()

        @pl.when(jnp.logical_not(early(i)))
        def _():
            @pl.when(jnp.logical_not(side_first(i)) | ((i > 3) & at_an_end))
            def _():
                for half in range(2):
                    wait_for(
                        dense.at[stream, part, plane, half],
                        dense_recv.at[stream, part, plane, half],
                    )

            for half in range(2):
                pltpu.make_async_copy(
                    dense.at[stream, part, plane, half], side.at[half], side_sem.at[half]
                ).start()

    def picks(i, number, rows_ref=routed_rows_ref):
        plane, stream, part = unit(i)
        owner, half, experts = targets[number]
        block = plane * PLANE + owner
        slot = lax.rem(i, 2)
        goal = rows_ref.at[block, :, columns(half, part)]
        sem = row_recv.at[stream, block, half, part]
        out = []
        for k in range(4):
            rows = picked.at[slot, number, pl.ds(k * capacity, capacity)]
            if k == 0:
                out.append(pltpu.make_async_copy(rows, goal, own_sem.at[slot, number]))
            else:
                out.append(push(rows, goal, row_send.at[slot, number, k], sem, z, experts[k]))
        return block, slot, experts, out

    def pick(i, number, source):
        block, slot, experts, sends = picks(i, number)

        @pl.when(i >= 2)
        def _():
            for send in sends[1:]:
                send.wait_send()

        select = one_hot(pos_ref, experts, block, capacity)
        picked[slot, number] = jnp.dot(select, source[...], preferred_element_type=f32).astype(low)
        for stream in range(2):

            @pl.when(unit(i)[1] == stream)
            def _():
                for send in picks(i, number, rows_refs[stream])[3]:
                    send.start()

    def wait_own(i, number):
        picks(i, number)[3][0].wait()

    def pair(c):
        plane = plane_of(lax.div(c, 4))
        j = lax.rem(c, 4)
        owner = (
            e + lax.rem(j, 2) * (here.x_same - e) + lax.div(j, 2) * (here.y_same - e)
        )
        first = plane * PLANE + owner
        at = owner * LINE + plane
        owners = (owner, owner + here.sib - e)
        return j, first, first + here.sib - e, (at, at + (here.sib - e) * LINE, plane, owners)

    def takes(c):
        _, first, second, _ = pair(c)
        slot = lax.rem(c, 2)
        return [
            pltpu.make_async_copy(
                rows_refs[stream].at[block],
                taken.at[slot, stream, pl.ds(number * capacity, capacity)],
                taken_sem.at[slot, stream, number],
            )
            for stream in range(2)
            for number, block in enumerate((first, second))
        ]

    def take(c):
        j, first, second, _ = pair(c)

        def wait_rows(block, half):
            for stream in range(2):
                for part in range(2):
                    wait_for(
                        rows_refs[stream].at[block, :, part_columns(half, part)],
                        row_recv.at[stream, block, half, part],
                    )

        for half in range(2):
            wait_rows(second, half)

        @pl.when((j == 2) | (j == 3))
        def _():
            wait_rows(first, 0)

        @pl.when((j == 1) | (j == 3))
        def _():
            wait_rows(first, 1)

        for copy in takes(c):
            copy.start()

    def puts(c):
        _, first, second, out_at = pair(c)
        out = []
        for number, block in enumerate((first, second)):
            at = pl.ds(number * capacity, capacity)
            for kind, (held, goal) in enumerate(
                (
                    (out_held.at[:, pl.ds(0, MODEL_WIDTH // 2)], out_ref),
                    (out_held.at[:, pl.ds(MODEL_WIDTH // 2, MODEL_WIDTH // 2)], out_second_ref),
                    (back_held, back_ref),
                    (act_held, act_ref),
                    (gate_held, gate_low_ref),
                    (up_held, up_low_ref),
                )
            ):
                to = out_at[number] if kind < 2 else block
                out.append(
                    pltpu.make_async_copy(held.at[at], goal.at[to], put_sem.at[kind, number])
                )
        return out

    def compute(c):
        for copy in takes(c):
            copy.wait()

        @pl.when(c > 0)
        def _():
            for copy in puts(c - 1):
                copy.wait()

        slot = lax.rem(c, 2)
        _, first, second, (_, _, plane, owners) = pair(c)
        slots = lax.broadcasted_iota(jnp.int32, (capacity, DEVICE_TOKENS), 0)
        chosen = [slots == pos_ref[e, pl.ds(block, 1), :] for block in (first, second)]
        gates = jnp.concatenate(
            [
                jnp.sum(
                    jnp.where(mask, gates_here[plane, owner], 0.0), axis=1, keepdims=True
                )
                for mask, owner in zip(chosen, owners)
            ],
            axis=0,
        )
        rows = taken[slot, 0]
        gate_part = jnp.dot(rows, w_gate_ref[...], preferred_element_type=f32)
        up_part = jnp.dot(rows, w_up_ref[...], preferred_element_type=f32)
        sigmoid = 1.0 / (1.0 + jnp.exp(-gate_part))
        silu = gate_part * sigmoid
        act_low = (silu * up_part).astype(low)
        pull = across(taken[slot, 1], w_down_ref[...], (1, 1))
        act = act_low.astype(f32)
        row_grad = jnp.sum(act * pull, axis=1, keepdims=True)
        for number, owner in enumerate(owners):
            mine = row_grad[number * capacity : (number + 1) * capacity]
            gate_grad_ref[plane, owner] = jnp.sum(
                jnp.where(chosen[number], mine, 0.0), axis=0, keepdims=True
            )
        act_held[...] = (act * gates).astype(low)
        pull = pull * gates
        gate_low = (pull * up_part * (sigmoid * (1.0 + gate_part * (1.0 - sigmoid)))).astype(low)
        up_low = (pull * silu).astype(low)
        gate_held[...] = gate_low
        up_held[...] = up_low
        out_held[...] = (
            jnp.dot(act_low, w_down_ref[...], preferred_element_type=f32) * gates
        ).astype(low)
        back_held[...] = (
            across(gate_low, w_gate_ref[...], (1, 1)) + across(up_low, w_up_ref[...], (1, 1))
        ).astype(low)
        for copy in puts(c):
            copy.start()

    def step(i, carry):
        @pl.when((i > 0) & (i <= UNITS))
        def _():
            wait_own(i - 1, 0)
            wait_own(i - 1, 1)

        @pl.when(i < UNITS)
        def _():
            for half in range(2):
                wait_for(near.at[half], near_sem.at[half])
                pick(i, half, near.at[half])

        @pl.when((i > 0) & (i <= UNITS))
        def _():
            for half in range(2):
                wait_for(side.at[half], side_sem.at[half])
                pick(i - 1, 2 + half, side.at[half])

        @pl.when(i < UNITS - 1)
        def _():
            arrive(i + 1)

        @pl.when(i < UNITS)
        def _():
            arrive_side(i)

        @pl.when(i == 1)
        def _():
            spread_gates()

        @pl.when(i == LAG)
        def _():
            wait_gates()

        @pl.when(i >= LAG)
        def _():
            @pl.when(lax.rem(i - LAG, 4) == 0)
            def _():
                take(i - LAG)

            compute(i - LAG)

        @pl.when((i > 0) & (i <= UNITS))
        def _():
            wait_own(i - 1, 2)
            wait_own(i - 1, 3)

        @pl.when((i >= LAG) & (lax.rem(i - LAG, 4) != 3))
        def _():
            take(i - (LAG - 1))

        for first_step, last_step, ahead in ((1, 4, 3), (2, 5, 6), (5, 8, 7)):

            @pl.when(
                (i >= first_step)
                & (i <= last_step)
                & jnp.logical_not(at_an_end)
                & jnp.logical_not(early(i + ahead))
            )
            def _():
                pass_on(i + ahead)

        @pl.when(i == 1)
        def _():
            pass_side_on(i + 2)

        for at_step, ahead in ((5, 2), (6, 5), (10, 5)):

            @pl.when((i == at_step) & jnp.logical_not(at_an_end))
            def _():
                pass_side_on(i + ahead)

        return carry

    for i in (0, 1, 3):
        pass_on(jnp.int32(i))
    for send in denses(jnp.int32(3)):
        send.start()
    arrive(jnp.int32(0))
    lax.fori_loop(0, UNITS + LAG, step, 0)
    for copy in puts(UNITS - 1):
        copy.wait()
    for move in gate_moves + gate_moves_on:
        move.wait_send()
    for i in (UNITS - 2, UNITS - 1):
        for number in range(4):
            for send in picks(jnp.int32(i), number)[3][1:]:
                send.wait_send()

    def drain(i, carry):
        @pl.when(jnp.logical_not(early(i)))
        def _():
            along(i, forwards(i), lambda send: send.wait_send())

            @pl.when(jnp.logical_not(side_first(i)) | (i == 3))
            def _():
                for send in denses(i):
                    send.wait_send()

        @pl.when(side_first(i))
        def _():
            along(i, side_forwards(i), lambda send: send.wait_send())

        return carry

    lax.fori_loop(0, UNITS, drain, 0)


def dispatch_and_expert(
    routed,
    cotangent,
    early_line,
    early_sides,
    positions,
    gates,
    w_gate,
    w_up,
    w_down,
    capacity,
    collective_id,
):
    low, f32 = jnp.bfloat16, jnp.float32
    blocks = LINE * PLANE
    dma = pltpu.SemaphoreType.DMA
    wide = jax.ShapeDtypeStruct((blocks, capacity, MODEL_WIDTH), low)
    half_wide = jax.ShapeDtypeStruct((blocks, capacity, MODEL_WIDTH // 2), low)
    narrow = jax.ShapeDtypeStruct((blocks, capacity, w_gate.shape[1]), low)
    landing = jax.ShapeDtypeStruct((2, 2, LINE, 2, DEVICE_TOKENS, PART), low)
    vmem = pl.BlockSpec(memory_space=pltpu.VMEM)
    anywhere = pl.BlockSpec(memory_space=pl.ANY)
    chunk = CHUNK * capacity
    return pl.pallas_call(
        expert_kernel,
        out_shape=[
            wide,
            wide,
            half_wide,
            half_wide,
            wide,
            narrow,
            narrow,
            narrow,
            jax.ShapeDtypeStruct(GATE_SHAPE, f32),
            landing,
            landing,
        ],
        in_specs=[vmem] * 5 + [anywhere] * 5,
        out_specs=[anywhere] * 8 + [vmem] + [anywhere] * 2,
        scratch_shapes=[
            pltpu.VMEM((2, DEVICE_TOKENS, MODEL_WIDTH), low),
            pltpu.VMEM((2, DEVICE_TOKENS, PART), low),
            pltpu.VMEM((2, DEVICE_TOKENS, PART), low),
            pltpu.VMEM(GATE_SHAPE, f32),
            pltpu.VMEM(GATE_SHAPE, f32),
            pltpu.VMEM((2, 4, 4 * capacity, PART), low),
            pltpu.VMEM((2, 2, chunk, MODEL_WIDTH), low),
            pltpu.VMEM((chunk, MODEL_WIDTH), low),
            pltpu.VMEM((chunk, MODEL_WIDTH), low),
            pltpu.VMEM((chunk, w_gate.shape[1]), low),
            pltpu.VMEM((chunk, w_gate.shape[1]), low),
            pltpu.VMEM((chunk, w_gate.shape[1]), low),
            dma((UNITS, 2, 2)),
            dma((2, 2, LINE, 2)),
            dma((UNITS, 2)),
            dma((2, 2, LINE, 2)),
            dma((LINE, 2, 2)),
            dma((2, 4, 4)),
            dma((2, blocks, 2, 2)),
            dma((2, 4)),
            dma((2,)),
            dma((2,)),
            dma((2, 2, 2)),
            dma((6, 2)),
            dma((LINE,)),
            dma((LINE,)),
            dma((PLANE,)),
            dma((PLANE,)),
        ],
        compiler_params=pltpu.CompilerParams(
            collective_id=collective_id, has_side_effects=True, vmem_limit_bytes=60 * 2**20
        ),
    )(positions, gates, w_gate, w_up, w_down, routed, cotangent, early_line, *early_sides)[:9]


def on_device(
    tokens,
    segments,
    routes,
    w_query,
    key_projection,
    value_projection,
    w_out,
    w_router,
    gain_attn,
    gain_ffn,
    gain_query,
    key_head_gain,
    w_gate,
    w_up,
    w_down,
    cotangent,
):
    f32 = jnp.float32
    brain_float = jnp.bfloat16
    sequence_length = tokens.shape[0]
    planes = lax.axis_size("fsdp")
    experts = planes * lax.axis_size("expert")
    capacity = 5 * DEVICE_TOKENS * TOP // (4 * experts)
    expert_ids = jnp.arange(experts, dtype=jnp.int32)
    my_expert = lax.axis_index("fsdp") * lax.axis_size("expert") + lax.axis_index("expert")
    in_blocks = (planes, experts) == (LINE, LINE * PLANE)

    small = (w_router, gain_attn, gain_ffn, gain_query, key_head_gain)
    small_sizes = [array.size for array in small]
    local_qkv = jnp.concatenate([w_query, key_projection, value_projection], axis=1)
    small_flat = jnp.concatenate([array.reshape(-1) for array in small])
    if in_blocks:
        width = -(-small_flat.size // (16 * 128)) * 128
        small_flat = jnp.pad(small_flat, (0, 16 * width - small_flat.size))
        cot_front = jnp.concatenate(
            [cotangent[:, :PART], cotangent[:, 2 * PART : 3 * PART]], axis=1
        )
        full_qkv, full_out, small_all, cot_line, routes_all = gather_all(
            (local_qkv, w_out), small_flat.reshape(16, width), cot_front, routes.T, 3
        )
        cot_line = cot_line.reshape(planes, sequence_length, 2 * PART)
        cot_sides = [
            lax.ppermute(
                cot_line[:, :, half * PART : (half + 1) * PART],
                "expert",
                [(device, device ^ (2 << half)) for device in range(PLANE)],
            )
            for half in range(2)
        ]
        small_all = small_all.reshape(planes, -1)
        routes_all = routes_all.reshape(experts, TOP, sequence_length)
    else:
        full_qkv = gather_shards(local_qkv)
        full_out = gather_shards(w_out)
        small_all = lax.all_gather(small_flat, "fsdp", axis=0)
    small_parts = []
    offset = 0
    for array, size in zip(small, small_sizes):
        part = small_all[:, offset : offset + size]
        small_parts.append(part.reshape((planes * array.shape[0],) + array.shape[1:]))
        offset += size
    full_router, attn_gain, ffn_gain, query_gain, key_gain = small_parts

    if in_blocks:
        plane_experts = lax.axis_index("fsdp") * PLANE + jnp.arange(PLANE, dtype=jnp.int32)
        plane_hits = jnp.any(routes_all[None] == plane_experts[:, None, None, None], axis=2)
        positions = ranks(plane_hits)
    else:
        hits = jnp.any(routes[None, :, :] == expert_ids[:, None, None], axis=-1)
        select = places(hits, capacity)
        cot_rows = jnp.einsum("brt,td->brd", select, cotangent, preferred_element_type=f32)
        cot_rows = lax.all_to_all(cot_rows.astype(brain_float), BOTH, 0, 0, tiled=True)

    inputs = tokens.astype(f32)
    normalized, norm_attn_back = jax.vjp(root_mean_norm, inputs, attn_gain.astype(f32))
    normed_low = normalized.astype(brain_float)
    qkv_raw = jnp.dot(normed_low, full_qkv, preferred_element_type=f32)
    cosine, sine = rope_tables(sequence_length, HEAD_SIZE)
    head_gains = (query_gain.astype(f32)[None, :], key_gain.astype(f32)[None, :])
    mixed_low, query_rot, key_rot, value_low, totals = attention(
        qkv_raw, segments, cosine, sine, *head_gains
    )
    hidden = inputs + jnp.dot(mixed_low, full_out, preferred_element_type=f32)
    routed, norm_ffn_back = jax.vjp(root_mean_norm, hidden, ffn_gain.astype(f32))
    routed_low = routed.astype(brain_float)
    logits = jnp.dot(routed_low, full_router, preferred_element_type=f32)
    chosen_mask = jnp.any(routes[:, :, None] == expert_ids[None, None, :], axis=1)

    def gating(logit_in):
        softmax_probs = jax.nn.softmax(logit_in, axis=-1)
        chosen = jnp.where(chosen_mask, softmax_probs, 0.0)
        return chosen / jnp.sum(chosen, axis=-1, keepdims=True)

    gates, gating_back = jax.vjp(gating, logits)
    flat = (experts * capacity, MODEL_WIDTH)
    if in_blocks:
        (
            rows,
            cot_rows,
            out_rows,
            out_second,
            rows_grad,
            act_low,
            gate_low,
            up_low,
            gate_grad,
        ) = dispatch_and_expert(
            routed_low,
            cotangent,
            cot_line,
            cot_sides,
            positions,
            gates.T.reshape(GATE_SHAPE),
            w_gate[0],
            w_up[0],
            w_down[0],
            capacity,
            1,
        )
    else:
        rows = jnp.einsum("brt,td->brd", select, routed_low, preferred_element_type=f32)
        rows = lax.all_to_all(rows.astype(brain_float), BOTH, 0, 0, tiled=True)
        here = lax.all_to_all(select, BOTH, 0, 0, tiled=True)
        gates_here = lax.all_to_all(gates.T, BOTH, 0, 0, tiled=True)
        row_gates = jnp.sum(here.astype(f32) * gates_here[:, None, :], axis=-1)
        (
            out_rows,
            rows_grad,
            row_gate_grad,
            gate_weight_grad,
            up_weight_grad,
            down_weight_grad,
        ) = expert_layer(
            rows.reshape(flat),
            cot_rows.reshape(flat),
            row_gates.reshape(-1),
            w_gate[0],
            w_up[0],
            w_down[0],
        )
        row_gate_grad = row_gate_grad.reshape(experts, capacity, 1)
        gate_grad = jnp.sum(here.astype(f32) * row_gate_grad, axis=1)

    def exchange_back(block, select_here):
        block = block.reshape(experts, capacity, MODEL_WIDTH)
        block = lax.all_to_all(block, BOTH, 0, 0, tiled=True)
        return jnp.einsum("brt,brd->td", select_here, block, preferred_element_type=f32)

    if in_blocks:
        routed_grad, gate_grad = combine(
            rows_grad.reshape(experts, capacity, MODEL_WIDTH), positions, gate_grad, 2
        )
        gate_grad = gate_grad.reshape(experts, sequence_length).T
        (
            out_rows,
            rows,
            cot_rows,
            act_low,
            gate_low,
            up_low,
            routed_grad,
        ) = lax.optimization_barrier(
            (out_rows, rows, cot_rows, act_low, gate_low, up_low, routed_grad)
        )

        def in_plane(block):
            return lax.all_to_all(
                block.reshape(PLANE, LINE, capacity, -1), "expert", 0, 0, tiled=True
            )

        gate_weight_grad, up_weight_grad = routed_weight_grads(
            rows.reshape(flat), gate_low.reshape(flat[0], -1), up_low.reshape(flat[0], -1)
        )

        def in_plane(block):
            return lax.all_to_all(
                block.reshape(PLANE, LINE, capacity, -1), "expert", 0, 0, tiled=True
            )

        returned = in_plane(out_rows)
        line_positions = lax.dynamic_index_in_dim(
            positions.reshape(PLANE, LINE, PLANE, sequence_length),
            lax.axis_index("expert"),
            axis=2,
            keepdims=False,
        )
        slots = jnp.arange(capacity, dtype=jnp.int32)
        line_select = (line_positions[:, :, None, :] == slots[:, None]).astype(brain_float)

        def sum_along(block):
            sums = jnp.einsum("ezct,ezcd->ztd", line_select, block, preferred_element_type=f32)
            sums = sums.astype(brain_float).reshape(-1, block.shape[-1])
            return lax.psum_scatter(sums, "fsdp", scatter_dimension=0, tiled=True), sums

    else:
        gate_grad = lax.all_to_all(gate_grad, BOTH, 0, 0, tiled=True).T
        routed_grad = exchange_back(rows_grad, select)
        result = hidden + exchange_back(out_rows, select)
    upstream = cotangent.astype(f32)
    logit_low = gating_back(gate_grad)[0].astype(brain_float)
    routed_grad = routed_grad + jnp.einsum(
        "se,de->sd", logit_low, full_router, preferred_element_type=f32
    )
    router_grad = jnp.einsum("sd,se->de", routed_low, logit_low, preferred_element_type=f32)
    hidden_grad, ffn_gain_grad = norm_ffn_back(routed_grad)
    hidden_grad = hidden_grad + upstream
    hidden_low = hidden_grad.astype(brain_float)
    mixture_gradient = jnp.einsum(
        "sd,ad->sa", hidden_low, full_out, preferred_element_type=f32
    ).astype(brain_float)
    query_pre, key_pre, value_pre, gain_grads = attention_back(
        qkv_raw,
        query_rot,
        key_rot,
        value_low,
        mixture_gradient,
        totals,
        segments,
        cosine,
        sine,
        *head_gains,
    )
    if in_blocks:
        (
            returned,
            out_second,
            query_pre,
            gate_weight_grad,
            up_weight_grad,
            cot_rows,
            act_low,
            mixed_low,
        ) = lax.optimization_barrier(
            (
                returned,
                out_second,
                query_pre,
                gate_weight_grad,
                up_weight_grad,
                cot_rows,
                act_low,
                mixed_low,
            )
        )
        down_weight_grad = down_weight_grads(
            cot_rows.reshape(flat), act_low.reshape(flat[0], -1)
        )
        result_first, _ = sum_along(returned)
        returned = in_plane(out_second)
    out_grad = jnp.einsum("sa,sd->ad", mixed_low, hidden_low, preferred_element_type=f32)
    qkv_pre = jnp.concatenate([query_pre, key_pre, value_pre], axis=1)
    qkv_weight_grad = jnp.einsum("sd,sa->da", normed_low, qkv_pre, preferred_element_type=f32)
    normed_grad = jnp.einsum("sa,da->sd", qkv_pre, full_qkv, preferred_element_type=f32)
    input_grad, attn_gain_grad = norm_attn_back(normed_grad)
    input_grad = (input_grad + hidden_grad).astype(brain_float)
    small_grads = [
        grad.reshape(planes, -1).astype(brain_float)
        for grad in (router_grad, attn_gain_grad, ffn_gain_grad, gain_grads[0], gain_grads[1])
    ]
    small_grads = jnp.concatenate(small_grads, axis=1)
    if in_blocks:
        lanes = 128
        width = -(-small_grads.shape[1] // (PLANE * 32 * lanes)) * (PLANE * 32 * lanes)
        small_grads = jnp.pad(small_grads, ((0, 0), (0, width - small_grads.shape[1])))
        qkv_low = qkv_weight_grad.astype(brain_float)
        out_low = out_grad.astype(brain_float)
        (
            returned,
            qkv_low,
            out_low,
            input_grad,
            gate_weight_grad,
            up_weight_grad,
            down_weight_grad,
        ) = lax.optimization_barrier(
            (
                returned,
                qkv_low,
                out_low,
                input_grad,
                gate_weight_grad,
                up_weight_grad,
                down_weight_grad,
            )
        )
        result_second, expert_sums = sum_along(returned)
        qkv_low, expert_sums = lax.optimization_barrier((qkv_low, expert_sums))
        qkv_sum, out_sum, small_sums = reduce_all(
            (qkv_low, out_low, small_grads.reshape(-1, lanes)), 4
        )
        qkv_sum, out_sum = qkv_sum.astype(f32), out_sum.astype(f32)
        result = hidden + jnp.concatenate([result_first, result_second], axis=1).astype(f32)
        small_sums = small_sums.reshape(-1).astype(f32)
    else:
        qkv_sum = scatter_sums(qkv_weight_grad.astype(brain_float))
        out_sum = scatter_sums(out_grad.astype(brain_float))
        small_sums = lax.psum(
            lax.psum_scatter(small_grads, "fsdp", scatter_dimension=0, tiled=True), "expert"
        ).astype(f32)[0]
    query_width = QUERY_HEADS * HEAD_SIZE
    key_width = query_width + KEY_VALUE_HEADS * HEAD_SIZE
    summed = [
        qkv_sum[:, :query_width],
        qkv_sum[:, query_width:key_width],
        qkv_sum[:, key_width:],
        out_sum,
    ]
    offset = 0
    for array, size in zip(small, small_sizes):
        summed.append(small_sums[offset : offset + size].reshape(array.shape))
        offset += size
    return (
        (result.astype(brain_float), input_grad)
        + tuple(summed)
        + (gate_weight_grad[None], up_weight_grad[None], down_weight_grad[None])
    )


def solution(mesh):
    in_specs = (
        P(("fsdp", "expert"), None),
        P(("fsdp", "expert"), None),
        P(("fsdp", "expert"), None),
        P("fsdp", None),
        P("fsdp", None),
        P("fsdp", None),
        P("fsdp", None),
        P("fsdp", None),
        P("fsdp"),
        P("fsdp"),
        P("fsdp"),
        P("fsdp"),
        P(("fsdp", "expert"), None, None),
        P(("fsdp", "expert"), None, None),
        P(("fsdp", "expert"), None, None),
        P(("fsdp", "expert"), None),
    )
    out_specs = (
        P(("fsdp", "expert"), None),
        P(("fsdp", "expert"), None),
        P("fsdp", None),
        P("fsdp", None),
        P("fsdp", None),
        P("fsdp", None),
        P("fsdp", None),
        P("fsdp"),
        P("fsdp"),
        P("fsdp"),
        P("fsdp"),
        P(("fsdp", "expert"), None, None),
        P(("fsdp", "expert"), None, None),
        P(("fsdp", "expert"), None, None),
    )
    return jax.shard_map(
        on_device, mesh=mesh, in_specs=in_specs, out_specs=out_specs, check_vma=False
    )
```

```python
import functools

import jax
import jax.numpy as jnp
from jax import lax
from jax.experimental import pallas as pl
from jax.experimental.pallas import tpu as pltpu
from jax.sharding import PartitionSpec as P

MODEL_WIDTH = 2048
QUERY_HEADS = 32
KEY_VALUE_HEADS = 4
HEAD_SIZE = 128
TOP = 8
DEVICE_TOKENS = 512


EPSILON = 1e-06
ROPE_BASE = 1000000.0


def root_mean_norm(values_in, gain_in):
    return (
        values_in
        * lax.rsqrt(jnp.mean(values_in * values_in, axis=-1, keepdims=True) + EPSILON)
        * gain_in
    )


def rope_tables(sequence_length, width):
    inverse = 1.0 / ROPE_BASE ** (jnp.arange(0, width, 2, dtype=jnp.float32) / width)
    angles = jnp.arange(sequence_length, dtype=jnp.float32)[:, None] * inverse[None, :]
    cosine, sine = jnp.cos(angles), jnp.sin(angles)
    return (
        jnp.concatenate([cosine, cosine], axis=-1),
        jnp.concatenate([-sine, sine], axis=-1),
    )


def swiglu(gate_in, up_in):
    return jax.nn.silu(gate_in) * up_in


BOTH = ("fsdp", "expert")


def gather_shards(shard):
    parts = lax.axis_size("expert")
    rows = shard.shape[0] // parts
    own = lax.dynamic_slice_in_dim(shard, lax.axis_index("expert") * rows, rows, axis=0)
    return lax.all_gather(own, BOTH, axis=0, tiled=True)


def scatter_sums(whole):
    part = lax.psum_scatter(whole, BOTH, scatter_dimension=0, tiled=True)
    return lax.all_gather(part, "expert", axis=0, tiled=True).astype(jnp.float32)


def routed_weight_grads(rows, gate_low, up_low):
    return tuple(
        jnp.einsum("rd,rf->df", rows, low, preferred_element_type=jnp.float32)
        for low in (gate_low, up_low)
    )


def down_weight_grads(row_cotangent, act_scaled):
    return jnp.einsum(
        "rf,rd->fd", act_scaled, row_cotangent, preferred_element_type=jnp.float32
    )


def expert_layer(rows, row_cotangent, row_gates, w_gate, w_up, w_down):
    f32 = jnp.float32
    low = jnp.bfloat16
    gate_part = jnp.dot(rows, w_gate, preferred_element_type=f32)
    up_part = jnp.dot(rows, w_up, preferred_element_type=f32)
    activation, swiglu_back = jax.vjp(swiglu, gate_part, up_part)
    act_low = activation.astype(low)
    out_rows = (
        jnp.dot(act_low, w_down, preferred_element_type=f32) * row_gates[:, None]
    ).astype(low)
    act_pull = jnp.einsum("rd,fd->rf", row_cotangent, w_down, preferred_element_type=f32)
    gate_grad = jnp.sum(act_low.astype(f32) * act_pull, axis=-1)
    act_scaled = (act_low.astype(f32) * row_gates[:, None]).astype(low)
    gate_part_grad, up_part_grad = swiglu_back(act_pull * row_gates[:, None])
    gate_low = gate_part_grad.astype(low)
    up_low = up_part_grad.astype(low)
    rows_grad = (
        jnp.einsum("rf,df->rd", gate_low, w_gate, preferred_element_type=f32)
        + jnp.einsum("rf,df->rd", up_low, w_up, preferred_element_type=f32)
    ).astype(low)
    weight_grads = routed_weight_grads(rows, gate_low, up_low)
    weight_grads += (down_weight_grads(row_cotangent, act_scaled),)
    return (out_rows, rows_grad, gate_grad) + weight_grads


def ranks(hits):
    length = hits.shape[-1]
    before = jnp.arange(length)[:, None] <= jnp.arange(length)[None, :]
    counts = jnp.einsum(
        "...s,st->...t",
        hits.astype(jnp.bfloat16),
        before.astype(jnp.bfloat16),
        preferred_element_type=jnp.float32,
    )
    return jnp.where(hits, counts.astype(jnp.int32) - 1, -1)


def places(hits, capacity):
    slots = jnp.arange(capacity, dtype=jnp.int32)
    return (ranks(hits)[..., None, :] == slots[:, None]).astype(jnp.bfloat16)


MESH = pl.DeviceIdType.MESH
LINE = 4
PLANE = 8
PART = 512
FAR_FIRST = (3, 0, 2, 1)


class Place:
    def __init__(self):
        self.z = lax.axis_index("fsdp")
        self.e = lax.axis_index("expert")
        core = lax.rem(self.e, 2)
        x = lax.rem(lax.div(self.e, 2), 2)
        y = lax.div(self.e, 4)
        self.sib = self.e + 1 - 2 * core
        self.x_same = self.e + 2 - 4 * x
        self.y_same = self.e + 4 - 8 * y
        self.d_same = self.x_same + 4 - 8 * y
        self.x_other = self.x_same + 1 - 2 * core
        self.y_other = self.y_same + 1 - 2 * core
        self.d_other = self.d_same + 1 - 2 * core
        self.plane = [lax.rem(self.e + k, PLANE) for k in range(1, PLANE)]
        self.line = [lax.rem(self.z + k, LINE) for k in range(1, LINE)]

    def greet(self):
        barrier = pltpu.get_barrier_semaphore()
        others = [(self.z, other) for other in self.plane] + [(other, self.e) for other in self.line]
        for z, e in others:
            pl.semaphore_signal(barrier, inc=1, device_id=(z, e), device_id_type=MESH)
        pl.semaphore_wait(barrier, len(others))


def push(source, target, send, recv, z, e):
    return pltpu.make_async_remote_copy(
        src_ref=source,
        dst_ref=target,
        send_sem=send,
        recv_sem=recv,
        device_id=(z, e),
        device_id_type=MESH,
    )


def part_columns(half, part):
    return pl.ds(half * 2 * PART + part * PART, PART)


def one_hot(pos_ref, experts, block, capacity):
    slots = lax.broadcasted_iota(jnp.int32, (capacity, DEVICE_TOKENS), 0)
    return jnp.concatenate(
        [
            (slots == pos_ref[expert, pl.ds(block, 1), :]).astype(jnp.float32)
            for expert in experts
        ],
        axis=0,
    ).astype(jnp.bfloat16)


def along_line(here, source, goal, send, recv):
    return [
        push(
            source.at[plane],
            goal.at[here.z],
            send.at[k],
            recv.at[here.z],
            plane,
            here.e,
        )
        for k, plane in enumerate(here.line)
    ]


def in_plane_of(here, source, goal, send, recv):
    return [
        push(
            source.at[:, owner],
            goal.at[:, here.e],
            send.at[k],
            recv.at[here.e],
            here.z,
            owner,
        )
        for k, owner in enumerate(here.plane)
    ]


def target_sets(here):
    with_y = (here.e, here.sib, here.y_same, here.y_other)
    with_x = (here.e, here.sib, here.x_same, here.x_other)
    return (
        (here.e, 0, with_y),
        (here.e, 1, with_x),
        (here.x_same, 0, with_y),
        (here.y_same, 1, with_x),
    )


CUTS = 4
CUT = 256
AHEAD = 2


def cut_columns(half, part):
    return pl.ds(half * CUTS * CUT + part * CUT, CUT)


def combine_kernel(
    pos_ref,
    gate_grad_ref,
    rows_ref,
    out_ref,
    gate_out_ref,
    gates_plane,
    held,
    dense_out,
    dense_in,
    sums,
    passed,
    held_send,
    held_recv,
    dense_send,
    dense_recv,
    pass_send,
    pass_recv,
    gate_plane_send,
    gate_plane_recv,
    gate_line_send,
    gate_line_recv,
):
    here = Place()
    z, e = here.z, here.e
    capacity = rows_ref.shape[1]
    here.greet()
    targets = target_sets(here)
    units = [(part, plane) for part in range(CUTS) for plane in FAR_FIRST]
    at_end = []

    def unit_of(part, plane):
        return part * LINE + plane

    def compact(index):
        part, plane = units[index]
        unit = unit_of(part, plane)

        def rows_of(owner, half):
            return rows_ref.at[plane * PLANE + owner, :, cut_columns(half, part)]

        def slot(number, k):
            return held.at[unit, number, pl.ds(k * capacity, capacity)]

        for number, owner, half in (
            (2, here.x_same, 0),
            (3, here.y_same, 1),
            (0, here.e, 0),
            (1, here.e, 1),
        ):
            pltpu.make_async_copy(
                rows_of(owner, half), slot(number, 0), held_recv.at[unit, number, 0]
            ).start()
        for count, (goal, number, k, owner, half) in enumerate(
            (
                (here.y_same, 2, 2, here.d_same, 0),
                (here.x_same, 3, 2, here.d_same, 1),
                (here.y_other, 2, 3, here.d_other, 0),
                (here.x_other, 3, 3, here.d_other, 1),
                (here.sib, 2, 1, here.x_other, 0),
                (here.sib, 3, 1, here.y_other, 1),
                (here.sib, 0, 1, here.sib, 0),
                (here.sib, 1, 1, here.sib, 1),
                (here.y_same, 0, 2, here.y_same, 0),
                (here.x_same, 1, 2, here.x_same, 1),
                (here.y_other, 0, 3, here.y_other, 0),
                (here.x_other, 1, 3, here.x_other, 1),
            )
        ):
            send = push(
                rows_of(owner, half),
                slot(number, k),
                held_send.at[unit, count],
                held_recv.at[unit, number, k],
                z,
                goal,
            )
            send.start()
            at_end.append((None, [send]))

    def put_together(index, number):
        part, plane = units[index]
        unit = unit_of(part, plane)
        owner, _, experts = targets[number]
        for k in range(4):
            wait_for(
                held.at[unit, number, pl.ds(k * capacity, capacity)],
                held_recv.at[unit, number, k],
            )
        select = one_hot(pos_ref, experts, plane * PLANE + owner, capacity)
        return lax.dot_general(
            select,
            held[unit, number],
            (((0,), (0,)), ((), ())),
            preferred_element_type=jnp.float32,
        )

    def first(index):
        part, plane = units[index]
        unit = unit_of(part, plane)
        slot = index % 4
        for half in range(2):
            send = push(
                dense_out.at[half, slot],
                dense_in.at[half, unit],
                dense_send.at[half, slot],
                dense_recv.at[half, unit],
                z,
                (here.x_same, here.y_same)[half],
            )
            if index >= 4:
                send.wait_send()
            dense_out[half, slot] = put_together(index, 2 + half).astype(jnp.bfloat16)
            send.start()
            if index >= len(units) - 4:
                at_end.append((None, [send]))

    def hand_on(index, plane_here, up):
        part, plane = units[index]
        unit = unit_of(part, plane)
        goal = plane_here + 1 if up else plane_here - 1
        slot = unit if up or goal != plane else CUTS * LINE + part
        send = push(
            sums.at[unit], passed.at[slot], pass_send.at[unit], pass_recv.at[slot], goal, e
        )
        send.start()
        return send

    def second(index):
        part, plane = units[index]
        unit = unit_of(part, plane)
        for half in range(2):
            wait_for(dense_in.at[half, unit], dense_recv.at[half, unit])
            whole = put_together(index, half) + dense_in[half, unit].astype(jnp.float32)
            sums[unit, :, half * CUT : (half + 1) * CUT] = whole.astype(jnp.bfloat16)
        if plane > 0:

            @pl.when(z == 0)
            def _():
                hand_on(index, 0, True)

        if plane < LINE - 1:

            @pl.when(z == LINE - 1)
            def _():
                hand_on(index, LINE - 1, False)

    def third(index, hop):
        part, plane = units[index]
        unit = unit_of(part, plane)
        ways = []
        if hop < plane and hop < LINE - 1:
            ways.append((hop, True))
        if LINE - 1 - hop > plane and LINE - 1 - hop > 0:
            ways.append((LINE - 1 - hop, False))
        for plane_here, up in ways:

            @pl.when(z == plane_here)
            def _():
                wait_for(passed.at[unit], pass_recv.at[unit])
                total = sums[unit].astype(jnp.float32) + passed[unit].astype(jnp.float32)
                sums[unit] = total.astype(jnp.bfloat16)
                hand_on(index, plane_here, up)

    own = pl.ds(e, 1)
    gates_plane[:, own] = gate_grad_ref[:, own]
    gate_moves = in_plane_of(here, gate_grad_ref, gates_plane, gate_plane_send, gate_plane_recv)
    gate_moves_on = along_line(here, gates_plane, gate_out_ref, gate_line_send, gate_line_recv)
    for move in gate_moves:
        move.start()

    count = len(units)
    for ahead in range(AHEAD):
        compact(ahead)
    for step in range(count + 3):
        if step + AHEAD < count:
            compact(step + AHEAD)
        if step == 2:
            for owner in here.plane:
                wait_for(gates_plane.at[:, owner], gate_plane_recv.at[owner])
            gate_out_ref[z] = gates_plane[z]
            for move in gate_moves_on:
                move.start()
        if step < count:
            first(step)
        if 0 <= step - 1 < count:
            second(step - 1)
        for hop in (1, 2):
            if 0 <= step - 1 - hop < count:
                third(step - 1 - hop, hop)

    for plane in here.line:
        wait_for(gate_out_ref.at[plane], gate_line_recv.at[plane])
    for move in gate_moves + gate_moves_on:
        move.wait_send()
    for part in range(CUTS):
        unit = part * LINE + z
        for half in range(2):
            out_ref[:, cut_columns(half, part)] = sums[
                unit, :, half * CUT : (half + 1) * CUT
            ].astype(jnp.float32)
        for going, slot in ((z > 0, unit), (z < LINE - 1, CUTS * LINE + part)):

            @pl.when(going)
            def _():
                wait_for(passed.at[slot], pass_recv.at[slot])
                for half in range(2):
                    columns = cut_columns(half, part)
                    out_ref[:, columns] = out_ref[:, columns] + passed[
                        slot, :, half * CUT : (half + 1) * CUT
                    ].astype(jnp.float32)

    for _, sends in at_end:
        for send in sends:
            send.wait_send()
    for part, plane in units:
        unit = unit_of(part, plane)

        @pl.when(z != plane)
        def _():
            push(
                sums.at[unit], passed.at[unit], pass_send.at[unit], pass_recv.at[unit], z, here.sib
            ).wait_send()


def combine(rows, positions, gate_grad, collective_id):
    capacity = rows.shape[1]
    bf16 = jnp.bfloat16
    dma = pltpu.SemaphoreType.DMA
    units = CUTS * LINE
    return pl.pallas_call(
        combine_kernel,
        out_shape=[
            jax.ShapeDtypeStruct((DEVICE_TOKENS, MODEL_WIDTH), jnp.float32),
            jax.ShapeDtypeStruct(GATE_SHAPE, jnp.float32),
        ],
        in_specs=[
            pl.BlockSpec(memory_space=pltpu.VMEM),
            pl.BlockSpec(memory_space=pltpu.VMEM),
            pl.BlockSpec(memory_space=pl.ANY),
        ],
        out_specs=[pl.BlockSpec(memory_space=pltpu.VMEM)] * 2,
        scratch_shapes=[
            pltpu.VMEM(GATE_SHAPE, jnp.float32),
            pltpu.VMEM((units, 4, 4 * capacity, CUT), bf16),
            pltpu.VMEM((2, 4, DEVICE_TOKENS, CUT), bf16),
            pltpu.VMEM((2, units, DEVICE_TOKENS, CUT), bf16),
            pltpu.VMEM((units, DEVICE_TOKENS, 2 * CUT), bf16),
            pltpu.VMEM((units + CUTS, DEVICE_TOKENS, 2 * CUT), bf16),
            dma((units, 12)),
            dma((units, 4, 4)),
            dma((2, 4)),
            dma((2, units)),
            dma((units,)),
            dma((units + CUTS,)),
            dma((PLANE,)),
            dma((PLANE,)),
            dma((LINE,)),
            dma((LINE,)),
        ],
        compiler_params=pltpu.CompilerParams(
            collective_id=collective_id, has_side_effects=True, vmem_limit_bytes=60 * 2**20
        ),
    )(positions, gate_grad, rows)


def near_first(z):
    power_of_four = (
        1 + 3 * z + lax.div(z * (z - 1), 2) * 9 + lax.div(z * (z - 1) * (z - 2), 6) * 27
    )
    orders = ((0, 1, 2, 3), (1, 0, 2, 3), (2, 3, 1, 0), (3, 2, 1, 0))
    tables = [
        sum(order[step] * 4**plane for plane, order in enumerate(orders)) for step in range(LINE)
    ]
    return [lax.rem(lax.div(jnp.int32(table), power_of_four), 4) for table in tables]


def wait_for(buffer, sem):
    pltpu.make_async_copy(buffer, buffer, sem).wait()


def spread_in_plane(here, whole, rows, halves, plane, recv, send, number, at_end, mine):
    z = here.z

    def piece(owner, half):
        start, size = halves[half]
        return whole.at[pl.ds((plane * PLANE + owner) * rows + start, size)]

    def to(owner, half, goal, count):
        copy = push(
            piece(owner, half),
            piece(owner, half),
            send.at[number, count],
            recv.at[plane * PLANE + owner, half],
            z,
            goal,
        )
        copy.start()
        at_end.append((None, [copy]))

    def arrived(owner, half):
        wait_for(piece(owner, half), recv.at[plane * PLANE + owner, half])

    ways = range(len(halves))

    def first():
        for half in ways:
            mine(half)
            to(here.e, half, here.x_same, 3 * half)
            to(here.e, half, here.y_same, 3 * half + 1)
            to(here.e, half, here.sib, 3 * half + 2)

    def second():
        for half in ways:
            arrived(here.x_same, half)
            if half == len(halves) - 1:
                to(here.x_same, half, here.y_same, 6)
            to(here.x_same, half, here.sib, 7 + half)
            arrived(here.y_same, half)
            if half == 0 and len(halves) > 1:
                to(here.y_same, half, here.x_same, 9)
            to(here.y_same, half, here.sib, 10 + half)

    def third():
        for half in ways:
            arrived(here.d_same, half)
            to(here.d_same, half, here.sib, 12 + half)

    def last():
        for owner in (here.sib, here.x_other, here.y_other, here.d_other):
            for half in ways:
                arrived(owner, half)

    return first, second, third, last


def finish(at_end):
    for go, sends in at_end:
        if go is None:
            for send in sends:
                send.wait_send()
        else:

            @pl.when(go)
            def _():
                for send in sends:
                    send.wait_send()


def halves_of(rows):
    return ((0, rows // 2), (rows // 2, rows // 2)) if rows >= 32 else ((0, rows),)


def gather_kernel(kinds, *refs):
    total = len(kinds)
    sources, wholes, scratch = refs[:total], refs[total : 2 * total], refs[2 * total :]
    here = Place()
    z, e = here.z, here.e
    here.greet()
    planes = near_first(z)
    at_end = []
    locals_ = []
    steps = [[] for _ in range(LINE)]
    arrays = []
    for index, (source, whole) in enumerate(zip(sources, wholes)):
        recv, send, line_send, own = scratch[4 * index : 4 * index + 4]
        passing = scratch[4 * total + index]
        kind = kinds[index]
        rows = source.shape[0] // (PLANE if kind == "weight" else 1)
        halves = halves_of(rows)
        arrays.append((kind, source, whole, rows, halves, recv, send, line_send))
        if kind == "block":
            base = (z * PLANE + e) * rows
        else:
            base = z * source.shape[0]
        first = pltpu.make_async_copy(source, passing, own.at[0])
        first.start()
        goal = whole.at[pl.ds(base, source.shape[0])]
        locals_.append((kind, first, pltpu.make_async_copy(passing, goal, own.at[1])))

    def line_piece(array, plane, half):
        kind, _, whole, rows, halves, _, _, _ = array
        start, size = halves[half]
        owner = plane if kind in ("plane", "late") else plane * PLANE + e
        return whole.at[pl.ds(owner * rows + start, size)]

    def line_sem(array, plane, half):
        owner = plane if array[0] in ("plane", "late") else plane * PLANE + e
        return array[5].at[owner, half]

    def along(array, step, half):
        plane = planes[step]
        kind, source, _, rows, halves, _, _, line_send = array
        for direction in range(2):
            if direction == 0:
                go = (plane <= z) & (z < LINE - 1)
                goal = z + 1
            else:
                go = (plane >= z) & (z > 0)
                goal = z - 1
            if step == 0:
                start, size = halves[half]
                offset = e * rows + start if kind == "weight" else start
                origin = source.at[pl.ds(offset, size)]
            else:
                origin = line_piece(array, plane, half)
            copy = push(
                origin,
                line_piece(array, plane, half),
                line_send.at[step, half, direction],
                line_sem(array, plane, half),
                goal,
                e,
            )

            @pl.when(go)
            def _():
                copy.start()

            at_end.append((go, [copy]))

    for array in arrays:
        if array[0] != "late":
            for half in range(len(array[4])):
                along(array, 0, half)
    for _, first, second in locals_:
        first.wait()
        second.start()
    for kind, _, second in locals_:
        if kind == "block":
            second.wait()

    later = []

    def arrive(step):
        work = []
        for array in arrays:
            kind, _, whole, rows, halves, recv, send, _ = array

            def mine(half, array=array):
                if step > 0:
                    wait_for(
                        line_piece(array, planes[step], half),
                        line_sem(array, planes[step], half),
                    )
                    along(array, step, half)

            if kind == "late":
                continue
            if kind == "plane" or (kind == "weight" and step == 0):
                if step > 0:
                    for half in range(len(halves)):
                        mine(half)
                continue
            first, second, third, last = spread_in_plane(
                here, whole, rows, halves, planes[step], recv, send, step, at_end, mine
            )
            first()
            work.append((second, third, last))
        later.append(work)

    def arrive_late(step):
        for array in arrays:
            if array[0] == "late":
                for half in range(len(array[4])):
                    if step > 0:
                        wait_for(
                            line_piece(array, planes[step], half),
                            line_sem(array, planes[step], half),
                        )
                    along(array, step, half)

    for step in range(LINE + 2):
        if step < LINE:
            arrive(step)
        if step >= 2:
            arrive_late(step - 2)
        if 0 <= step - 1 < LINE:
            for second, _, _ in later[step - 1]:
                second()
        if 0 <= step - 2 < LINE:
            for _, third, _ in later[step - 2]:
                third()
    for work in later:
        for _, _, last in work:
            last()
    for kind, _, second in locals_:
        if kind != "block":
            second.wait()
    finish(at_end)


def gather_all(weights, line, late, block, collective_id):
    sources = tuple(weights) + (line, late, block)
    kinds = ("weight",) * len(weights) + ("plane", "late", "block")
    parts = [LINE] * (len(sources) - 1) + [LINE * PLANE]
    dma = pltpu.SemaphoreType.DMA
    scratch = []
    for _ in sources:
        scratch += [dma((LINE * PLANE, 2)), dma((LINE, 16)), dma((LINE, 2, 2)), dma((2,))]
    scratch += [pltpu.VMEM(array.shape, array.dtype) for array in sources]
    return pl.pallas_call(
        functools.partial(gather_kernel, kinds),
        out_shape=[
            jax.ShapeDtypeStruct((array.shape[0] * part,) + array.shape[1:], array.dtype)
            for array, part in zip(sources, parts)
        ],
        in_specs=[pl.BlockSpec(memory_space=pl.ANY)] * len(sources),
        out_specs=[pl.BlockSpec(memory_space=pl.ANY)] * len(sources),
        scratch_shapes=scratch,
        compiler_params=pltpu.CompilerParams(
            collective_id=collective_id, has_side_effects=True, vmem_limit_bytes=32 * 2**20
        ),
    )(*sources)


def add_into(goal, *terms):
    rows, columns = goal.shape

    def some(index, carry):
        at = pl.ds(pl.multiple_of(index * 16, 16), 16)
        for start in range(0, columns, 1024):
            cut = slice(start, start + 1024)
            total = goal[at, cut].astype(jnp.float32)
            for term in terms:
                total = total + term[at, cut].astype(jnp.float32)
            goal[at, cut] = total.astype(goal.dtype)
        return carry

    lax.fori_loop(0, rows // 16, some, 0)


def reduce_kernel(count, *refs):
    sources, wholes, scratch = refs[:count], refs[count : 2 * count], refs[2 * count :]
    here = Place()
    z, e = here.z, here.e
    here.greet()
    at_end = []
    owners = (here.d_same, here.x_same, here.y_same, here.e)
    other_owners = (here.d_other, here.x_other, here.y_other, here.sib)
    units = [(plane, index) for index in range(count) for plane in FAR_FIRST]
    names = (
        "held", "sib", "half", "side", "passed",
        "held_recv", "sib_recv", "sib_send", "half_recv", "half_send",
        "side_recv", "side_send", "pass_recv", "pass_send", "own", "out_recv", "out_send",
    )
    per = len(names)
    buffers = [dict(zip(names, scratch[per * i : per * i + per])) for i in range(count)]
    rows_of = [source.shape[0] // (LINE * PLANE) for source in sources]

    def sent(copy):
        copy.start()
        at_end.append((None, [copy]))

    def load(number):
        plane, index = units[number]
        b, rows, source = buffers[index], rows_of[index], sources[index]
        for kind in range(4):
            mine = source.at[pl.ds((plane * PLANE + owners[kind]) * rows, rows)]
            theirs = source.at[pl.ds((plane * PLANE + other_owners[kind]) * rows, rows)]
            sent(
                push(
                    theirs,
                    b["sib"].at[plane, kind],
                    b["sib_send"].at[plane, kind],
                    b["sib_recv"].at[plane, kind],
                    z,
                    here.sib,
                )
            )
            pltpu.make_async_copy(
                mine, b["held"].at[plane, kind], b["held_recv"].at[plane, kind]
            ).start()

    def both(number, kind):
        plane, index = units[number]
        b = buffers[index]
        wait_for(b["held"].at[plane, kind], b["held_recv"].at[plane, kind])
        wait_for(b["sib"].at[plane, kind], b["sib_recv"].at[plane, kind])
        add_into(b["held"].at[plane, kind], b["sib"].at[plane, kind])

    def first(number):
        plane, index = units[number]
        b, rows = buffers[index], rows_of[index]
        both(number, 0)
        for half, goal in enumerate((here.y_same, here.x_same)):
            at = pl.ds(half * rows // 2, rows // 2)
            sent(
                push(
                    b["held"].at[plane, 0, at],
                    b["half"].at[plane, at],
                    b["half_send"].at[plane, half],
                    b["half_recv"].at[plane, half],
                    z,
                    goal,
                )
            )
        both(number, 1)
        both(number, 2)

    def second(number):
        plane, index = units[number]
        b, rows = buffers[index], rows_of[index]
        for half, goal in enumerate((here.x_same, here.y_same)):
            at = pl.ds(half * rows // 2, rows // 2)
            wait_for(b["half"].at[plane, at], b["half_recv"].at[plane, half])
            add_into(b["held"].at[plane, 1 + half, at], b["half"].at[plane, at])
            sent(
                push(
                    b["held"].at[plane, 1 + half],
                    b["side"].at[half, plane],
                    b["side_send"].at[half, plane],
                    b["side_recv"].at[half, plane],
                    z,
                    goal,
                )
            )
        both(number, 3)

    def hand_on(number, plane_here, up):
        plane, index = units[number]
        b = buffers[index]
        goal = plane_here + 1 if up else plane_here - 1
        slot = plane if up or goal != plane else LINE
        push(
            b["held"].at[plane, 3],
            b["passed"].at[slot],
            b["pass_send"].at[plane],
            b["pass_recv"].at[slot],
            goal,
            e,
        ).start()

    def third(number):
        plane, index = units[number]
        b = buffers[index]
        for half in range(2):
            wait_for(b["side"].at[half, plane], b["side_recv"].at[half, plane])
        add_into(b["held"].at[plane, 3], b["side"].at[0, plane], b["side"].at[1, plane])
        if plane > 0:

            @pl.when(z == 0)
            def _():
                hand_on(number, 0, True)

        if plane < LINE - 1:

            @pl.when(z == LINE - 1)
            def _():
                hand_on(number, LINE - 1, False)

    def hop(number, distance):
        plane, index = units[number]
        b = buffers[index]
        ways = []
        if distance < plane and distance < LINE - 1:
            ways.append((distance, True))
        if LINE - 1 - distance > plane and LINE - 1 - distance > 0:
            ways.append((LINE - 1 - distance, False))
        for plane_here, up in ways:

            @pl.when(z == plane_here)
            def _():
                wait_for(b["passed"].at[plane], b["pass_recv"].at[plane])
                add_into(b["held"].at[plane, 3], b["passed"].at[plane])
                hand_on(number, plane_here, up)

    def spread(index):
        b, rows, whole = buffers[index], rows_of[index], wholes[index]
        for going, slot in ((z > 0, z), (z < LINE - 1, LINE)):

            @pl.when(going)
            def _():
                wait_for(b["passed"].at[slot], b["pass_recv"].at[slot])
                add_into(b["held"].at[z, 3], b["passed"].at[slot])

        copy = pltpu.make_async_copy(
            b["held"].at[z, 3], whole.at[pl.ds(e * rows, rows)], b["own"].at[0]
        )
        copy.start()
        copy.wait()
        return spread_in_plane(
            here,
            whole,
            rows,
            halves_of(rows),
            0,
            b["out_recv"],
            b["out_send"],
            0,
            at_end,
            lambda half: None,
        )

    steps = len(units)
    ready = LINE - 1 + 2 + 3
    spreads = {}
    load(0)
    load(1)
    for step in range((count - 1) * LINE + ready + 3):
        if step + 2 < steps:
            load(step + 2)
        if step < steps:
            first(step)
        if 0 <= step - 1 < steps:
            second(step - 1)
        if 0 <= step - 2 < steps:
            third(step - 2)
        for distance in (1, 2):
            if 0 <= step - 2 - distance < steps:
                hop(step - 2 - distance, distance)
        for index in range(count):
            stage = step - index * LINE - ready
            if stage == 0:
                spreads[index] = spread(index)
            if 0 <= stage < 3:
                spreads[index][stage]()
    for index in range(count):
        spreads[index][3]()
    finish(at_end)
    for plane, index in units:
        b = buffers[index]

        @pl.when(z != plane)
        def _():
            push(
                b["held"].at[plane, 3],
                b["passed"].at[plane],
                b["pass_send"].at[plane],
                b["pass_recv"].at[plane],
                z,
                here.sib,
            ).wait_send()


def reduce_all(arrays, collective_id):
    dma = pltpu.SemaphoreType.DMA
    scratch = []
    for array in arrays:
        rows = array.shape[0] // (LINE * PLANE)
        block = (rows, array.shape[1])
        scratch += [
            pltpu.VMEM((LINE, 4) + block, array.dtype),
            pltpu.VMEM((LINE, 4) + block, array.dtype),
            pltpu.VMEM((LINE,) + block, array.dtype),
            pltpu.VMEM((2, LINE) + block, array.dtype),
            pltpu.VMEM((LINE + 1,) + block, array.dtype),
            dma((LINE, 4)),
            dma((LINE, 4)),
            dma((LINE, 4)),
            dma((LINE, 2)),
            dma((LINE, 2)),
            dma((2, LINE)),
            dma((2, LINE)),
            dma((LINE + 1,)),
            dma((LINE,)),
            dma((1,)),
            dma((PLANE, 2)),
            dma((1, 16)),
        ]
    return pl.pallas_call(
        functools.partial(reduce_kernel, len(arrays)),
        out_shape=[
            jax.ShapeDtypeStruct((array.shape[0] // LINE, array.shape[1]), array.dtype)
            for array in arrays
        ],
        in_specs=[pl.BlockSpec(memory_space=pl.ANY)] * len(arrays),
        out_specs=[pl.BlockSpec(memory_space=pl.ANY)] * len(arrays),
        scratch_shapes=scratch,
        compiler_params=pltpu.CompilerParams(
            collective_id=collective_id, has_side_effects=True, vmem_limit_bytes=60 * 2**20
        ),
    )(*arrays)


ROWS = 256
FORWARD_ROWS = 256
LOG2_E = 1.4426950408889634
GROUP = QUERY_HEADS // KEY_VALUE_HEADS
SCORE_SCALE = HEAD_SIZE ** (-0.5)


def across(left, right, contract):
    return lax.dot_general(
        left, right, ((contract[:1], contract[1:]), ((), ())), preferred_element_type=jnp.float32
    )


def head_norm(raw, gain):
    scale = lax.rsqrt(jnp.mean(raw * raw, axis=-1, keepdims=True) + EPSILON)
    unit = raw * scale
    return scale, unit, unit * gain


def turned(rows, sine):
    return pltpu.roll(rows, HEAD_SIZE // 2, 1) * sine


def masked(segment_column, segment_row):
    shape = (segment_column.shape[0], segment_row.shape[1])
    before = lax.broadcasted_iota(jnp.int32, shape, 1) <= lax.broadcasted_iota(jnp.int32, shape, 0)
    return jnp.where(before & (segment_column == segment_row), 0.0, -1e30)


def row_blocks(length, rows=ROWS):
    return [(start, start + rows) for start in range(0, length, rows)]


def attention_kernel(
    query_ref,
    key_ref,
    value_ref,
    cosine_ref,
    sine_ref,
    query_gain_ref,
    key_gain_ref,
    column_ref,
    row_ref,
    mixed_ref,
    query_rot_ref,
    key_rot_ref,
    value_low_ref,
    total_ref,
    bias,
):
    low = jnp.bfloat16
    length = bias.shape[0]

    @pl.when(pl.program_id(0) == 0)
    def _():
        bias[...] = masked(column_ref[...], row_ref[...])

    cosine, sine = cosine_ref[...], sine_ref[...]
    _, _, key = head_norm(key_ref[...], key_gain_ref[...])
    key_rot = (key * cosine + turned(key, sine)).astype(low)
    key_rot_ref[...] = key_rot
    value = value_ref[...].astype(low)
    value_low_ref[...] = value
    totals = []
    for head in range(GROUP):
        columns = slice(head * HEAD_SIZE, (head + 1) * HEAD_SIZE)
        _, _, query = head_norm(query_ref[:, columns], query_gain_ref[...])
        query_rot = (query * cosine + turned(query, sine)).astype(low)
        query_rot_ref[:, columns] = query_rot
        parts = []
        for start, end in row_blocks(length, FORWARD_ROWS):
            scores = across(query_rot[start:end], key_rot[:end], (1, 1)) + bias[start:end, :end]
            peak = jnp.max(scores, axis=-1, keepdims=True)
            weights = jnp.exp2((scores - peak) * (SCORE_SCALE * LOG2_E))
            total = jnp.sum(weights, axis=-1, keepdims=True)
            mixed = across(weights.astype(low), value[:end], (1, 0)) * (1.0 / total)
            mixed_ref[start:end, columns] = mixed.astype(low)
            parts.append(peak * SCORE_SCALE + jnp.log(total))
        totals.append(jnp.concatenate(parts, axis=0))
    total_ref[0] = jnp.concatenate(totals, axis=1)


def attention(qkv, segments, cosine, sine, query_gain, key_gain):
    length = qkv.shape[0]
    width = GROUP * HEAD_SIZE
    low = jnp.bfloat16
    whole = lambda *shape: pl.BlockSpec(shape, lambda j: (0,) * len(shape))
    heads = lambda first: pl.BlockSpec((length, HEAD_SIZE), lambda j: (0, first + j))
    key_start = QUERY_HEADS
    return pl.pallas_call(
        attention_kernel,
        grid=(KEY_VALUE_HEADS,),
        in_specs=[
            pl.BlockSpec((length, width), lambda j: (0, j)),
            heads(key_start),
            heads(key_start + KEY_VALUE_HEADS),
            whole(length, HEAD_SIZE),
            whole(length, HEAD_SIZE),
            whole(1, HEAD_SIZE),
            whole(1, HEAD_SIZE),
            whole(length, 1),
            whole(1, length),
        ],
        out_specs=[
            pl.BlockSpec((length, width), lambda j: (0, j)),
            pl.BlockSpec((length, width), lambda j: (0, j)),
            heads(0),
            heads(0),
            pl.BlockSpec((1, length, GROUP), lambda j: (j, 0, 0)),
        ],
        out_shape=[
            jax.ShapeDtypeStruct((length, QUERY_HEADS * HEAD_SIZE), low),
            jax.ShapeDtypeStruct((length, QUERY_HEADS * HEAD_SIZE), low),
            jax.ShapeDtypeStruct((length, KEY_VALUE_HEADS * HEAD_SIZE), low),
            jax.ShapeDtypeStruct((length, KEY_VALUE_HEADS * HEAD_SIZE), low),
            jax.ShapeDtypeStruct((KEY_VALUE_HEADS, length, GROUP), jnp.float32),
        ],
        scratch_shapes=[pltpu.VMEM((length, length), jnp.float32)],
        compiler_params=pltpu.CompilerParams(vmem_limit_bytes=48 * 2**20),
    )(qkv, qkv, qkv, cosine, sine, query_gain, key_gain, segments.T, segments)


def attention_back_kernel(
    query_ref,
    key_ref,
    query_rot_ref,
    key_rot_ref,
    value_ref,
    mixed_grad_ref,
    total_ref,
    cosine_ref,
    sine_ref,
    query_gain_ref,
    key_gain_ref,
    column_ref,
    row_ref,
    query_out_ref,
    key_out_ref,
    value_out_ref,
    gains_ref,
    bias,
):
    low = jnp.bfloat16
    length = bias.shape[0]

    @pl.when(pl.program_id(0) == 0)
    def _():
        bias[...] = masked(column_ref[...], row_ref[...])
        gains_ref[...] = jnp.zeros_like(gains_ref)

    cosine, sine = cosine_ref[...], sine_ref[...]
    key_rot, value = key_rot_ref[...], value_ref[...]

    def before_norm(grad_rot, raw, gain):
        grad = grad_rot * cosine - turned(grad_rot, sine)
        scale, unit, _ = head_norm(raw, gain)
        gain_grad = jnp.sum(grad * unit, axis=0, keepdims=True)
        pulled = grad * gain
        back = scale * (pulled - unit * jnp.mean(pulled * unit, axis=-1, keepdims=True))
        return back.astype(low), gain_grad

    blocks = row_blocks(length)
    key_grads = [jnp.zeros((ROWS, HEAD_SIZE), jnp.float32) for _ in blocks]
    value_grads = [jnp.zeros((ROWS, HEAD_SIZE), jnp.float32) for _ in blocks]
    query_gain_grad = jnp.zeros((1, HEAD_SIZE), jnp.float32)
    for head in range(GROUP):
        columns = slice(head * HEAD_SIZE, (head + 1) * HEAD_SIZE)
        query_rot = query_rot_ref[:, columns]
        mixed_grad = mixed_grad_ref[:, columns]
        total = total_ref[0, :, head : head + 1]
        parts = []
        for start, end in blocks:
            scores = across(query_rot[start:end], key_rot[:end], (1, 1)) * SCORE_SCALE
            probs = jnp.exp(scores + bias[start:end, :end] - total[start:end])
            prob_grad = across(mixed_grad[start:end], value[:end], (1, 1))
            weighted = prob_grad * probs
            row_sum = jnp.sum(weighted, axis=-1, keepdims=True)
            score_low = (weighted - probs * row_sum).astype(low)
            probs_low = probs.astype(low)
            parts.append(across(score_low, key_rot[:end], (1, 0)) * SCORE_SCALE)
            key_part = across(score_low, query_rot[start:end], (0, 0))
            value_part = across(probs_low, mixed_grad[start:end], (0, 0))
            for index, (first, last) in enumerate(blocks):
                if last <= end:
                    key_grads[index] = key_grads[index] + key_part[first:last]
                    value_grads[index] = value_grads[index] + value_part[first:last]
        back, gain_grad = before_norm(
            jnp.concatenate(parts, axis=0), query_ref[:, columns], query_gain_ref[...]
        )
        query_out_ref[:, columns] = back
        query_gain_grad = query_gain_grad + gain_grad
    back, key_gain_grad = before_norm(
        jnp.concatenate(key_grads, axis=0) * SCORE_SCALE, key_ref[...], key_gain_ref[...]
    )
    key_out_ref[...] = back
    value_out_ref[...] = jnp.concatenate(value_grads, axis=0).astype(low)
    gains_ref[0:1] += query_gain_grad
    gains_ref[1:2] += key_gain_grad


def attention_back(
    qkv, query_rot, key_rot, value, mixed_grad, totals, segments, cosine, sine, query_gain, key_gain
):
    length = qkv.shape[0]
    width = GROUP * HEAD_SIZE
    low = jnp.bfloat16
    whole = lambda *shape: pl.BlockSpec(shape, lambda j: (0,) * len(shape))
    heads = lambda first: pl.BlockSpec((length, HEAD_SIZE), lambda j: (0, first + j))
    wide = pl.BlockSpec((length, width), lambda j: (0, j))
    return pl.pallas_call(
        attention_back_kernel,
        grid=(KEY_VALUE_HEADS,),
        in_specs=[
            wide,
            heads(QUERY_HEADS),
            wide,
            heads(0),
            heads(0),
            wide,
            pl.BlockSpec((1, length, GROUP), lambda j: (j, 0, 0)),
            whole(length, HEAD_SIZE),
            whole(length, HEAD_SIZE),
            whole(1, HEAD_SIZE),
            whole(1, HEAD_SIZE),
            whole(length, 1),
            whole(1, length),
        ],
        out_specs=[wide, heads(0), heads(0), whole(8, HEAD_SIZE)],
        out_shape=[
            jax.ShapeDtypeStruct((length, QUERY_HEADS * HEAD_SIZE), low),
            jax.ShapeDtypeStruct((length, KEY_VALUE_HEADS * HEAD_SIZE), low),
            jax.ShapeDtypeStruct((length, KEY_VALUE_HEADS * HEAD_SIZE), low),
            jax.ShapeDtypeStruct((8, HEAD_SIZE), jnp.float32),
        ],
        scratch_shapes=[pltpu.VMEM((length, length), jnp.float32)],
        compiler_params=pltpu.CompilerParams(vmem_limit_bytes=56 * 2**20),
    )(
        qkv,
        qkv,
        query_rot,
        key_rot,
        value,
        mixed_grad,
        totals,
        cosine,
        sine,
        query_gain,
        key_gain,
        segments.T,
        segments,
    )


UNITS = 16
FIRST_COLUMNS = 1152
GATE_SHAPE = (LINE, PLANE, 1, DEVICE_TOKENS)
LAG = 4
CHUNK = 2


def expert_kernel(
    pos_ref,
    gates_ref,
    w_gate_ref,
    w_up_ref,
    w_down_ref,
    routed_ref,
    cotangent_ref,
    early_line_ref,
    early_x_ref,
    early_y_ref,
    routed_rows_ref,
    cotangent_rows_ref,
    out_ref,
    out_second_ref,
    back_ref,
    act_ref,
    gate_low_ref,
    up_low_ref,
    gate_grad_ref,
    line,
    dense,
    own_held,
    near,
    side,
    gates_line,
    gates_here,
    picked,
    taken,
    out_held,
    back_held,
    act_held,
    gate_held,
    up_held,
    line_send,
    line_recv,
    dense_send,
    dense_recv,
    side_send,
    row_send,
    row_recv,
    own_sem,
    near_sem,
    side_sem,
    taken_sem,
    put_sem,
    gate_line_send,
    gate_line_recv,
    gate_plane_send,
    gate_plane_recv,
):
    here = Place()
    z, e = here.z, here.e
    capacity = out_ref.shape[1]
    low, f32 = jnp.bfloat16, jnp.float32
    rows_refs = (routed_rows_ref, cotangent_rows_ref)
    here.greet()
    targets = target_sets(here)
    planes = near_first(z)
    packed = planes[0] + 4 * planes[1] + 16 * planes[2] + 64 * planes[3]
    inputs = (routed_ref, cotangent_ref)

    def plane_of(step):
        power = (
            1
            + 3 * step
            + lax.div(step * (step - 1), 2) * 9
            + lax.div(step * (step - 1) * (step - 2), 6) * 27
        )
        return lax.rem(lax.div(packed, power), 4)

    def unit(i):
        return plane_of(lax.div(i, 4)), lax.rem(lax.div(i, 2), 2), lax.rem(i, 2)

    def columns(half, part):
        return pl.ds(pl.multiple_of(half * 2 * PART + part * PART, PART), PART)

    firsts = [
        pltpu.make_async_copy(inputs[stream], own_held.at[stream], near_sem.at[stream])
        for stream in range(2)
    ]
    for first in firsts:
        first.start()
    for stream in range(2):
        firsts[stream].wait()
        for part in range(stream, 2):
            for half in range(2):
                pltpu.make_async_copy(
                    own_held.at[stream, :, part_columns(half, part)],
                    line.at[stream, part, z, half],
                    line_recv.at[stream, part, z, half],
                ).start()
    at_an_end = (z == 0) | (z == LINE - 1)
    gates_line[z] = gates_ref[z]
    gate_moves = along_line(here, gates_ref, gates_line, gate_line_send, gate_line_recv)
    gate_moves_on = in_plane_of(here, gates_line, gates_here, gate_plane_send, gate_plane_recv)
    for move in gate_moves:
        move.start()

    def spread_gates():
        for plane in here.line:
            wait_for(gates_line.at[plane], gate_line_recv.at[plane])
        own = pl.ds(e, 1)
        gates_here[:, own] = gates_line[:, own]
        for move in gate_moves_on:
            move.start()

    def wait_gates():
        for owner in here.plane:
            wait_for(gates_here.at[:, owner], gate_plane_recv.at[owner])

    def forwards(i):
        plane, stream, part = unit(i)
        out = []
        for half in range(2):
            for direction in range(2):
                goal = z + 1 - 2 * direction
                out.append(
                    push(
                        line.at[stream, part, plane, half],
                        line.at[stream, part, plane, half],
                        line_send.at[i, half, direction],
                        line_recv.at[stream, part, plane, half],
                        goal,
                        e,
                    )
                )
        return out

    def side_forwards(i):
        plane, stream, part = unit(i)
        return [
            push(
                dense.at[stream, part, plane, half],
                dense.at[stream, part, plane, half],
                side_send.at[lax.div(i, 4), half, direction],
                dense_recv.at[stream, part, plane, half],
                z + 1 - 2 * direction,
                e,
            )
            for half in range(2)
            for direction in range(2)
        ]

    def along(i, sends, act):
        plane = unit(i)[0]

        @pl.when((plane <= z) & (z < LINE - 1))
        def _():
            act(sends[0])
            act(sends[2])

        @pl.when((plane >= z) & (z > 0))
        def _():
            act(sends[1])
            act(sends[3])

    def side_first(i):
        return lax.rem(i, 4) == 3

    def early(i):
        return lax.rem(i, 4) == 2

    def denses(i):
        plane, stream, part = unit(i)
        return [
            push(
                line.at[stream, part, plane, half],
                dense.at[stream, part, plane, half],
                dense_send.at[i, half],
                dense_recv.at[stream, part, plane, half],
                z,
                (here.x_same, here.y_same)[half],
            )
            for half in range(2)
        ]

    def pass_on(i):
        plane, stream, part = unit(i)
        for half in range(2):
            wait_for(line.at[stream, part, plane, half], line_recv.at[stream, part, plane, half])
        along(i, forwards(i), lambda send: send.start())

    def pass_side_on(i):
        plane, stream, part = unit(i)
        for half in range(2):
            wait_for(dense.at[stream, part, plane, half], dense_recv.at[stream, part, plane, half])
        along(i, side_forwards(i), lambda send: send.start())

    def arrive(i):
        plane, stream, part = unit(i)

        @pl.when(early(i))
        def _():
            for half in range(2):
                pltpu.make_async_copy(
                    early_line_ref.at[plane, :, pl.ds(half * PART, PART)],
                    near.at[half],
                    near_sem.at[half],
                ).start()

        @pl.when(jnp.logical_not(early(i)))
        def _():
            @pl.when((i >= 4) & at_an_end)
            def _():
                for half in range(2):
                    wait_for(
                        line.at[stream, part, plane, half], line_recv.at[stream, part, plane, half]
                    )

            for half in range(2):
                pltpu.make_async_copy(
                    line.at[stream, part, plane, half], near.at[half], near_sem.at[half]
                ).start()

            @pl.when(jnp.logical_not(side_first(i)))
            def _():
                for send in denses(i):
                    send.start()

    def arrive_side(i):
        plane, stream, part = unit(i)

        @pl.when(early(i))
        def _():
            for half, source in enumerate((early_x_ref, early_y_ref)):
                pltpu.make_async_copy(source.at[plane], side.at[half], side_sem.at[half]).start()

        @pl.when(jnp.logical_not(early(i)))
        def _():
            @pl.when(jnp.logical_not(side_first(i)) | ((i > 3) & at_an_end))
            def _():
                for half in range(2):
                    wait_for(
                        dense.at[stream, part, plane, half],
                        dense_recv.at[stream, part, plane, half],
                    )

            for half in range(2):
                pltpu.make_async_copy(
                    dense.at[stream, part, plane, half], side.at[half], side_sem.at[half]
                ).start()

    def picks(i, number, rows_ref=routed_rows_ref):
        plane, stream, part = unit(i)
        owner, half, experts = targets[number]
        block = plane * PLANE + owner
        slot = lax.rem(i, 2)
        goal = rows_ref.at[block, :, columns(half, part)]
        sem = row_recv.at[stream, block, half, part]
        out = []
        for k in range(4):
            rows = picked.at[slot, number, pl.ds(k * capacity, capacity)]
            if k == 0:
                out.append(pltpu.make_async_copy(rows, goal, own_sem.at[slot, number]))
            else:
                out.append(push(rows, goal, row_send.at[slot, number, k], sem, z, experts[k]))
        return block, slot, experts, out

    def pick(i, number, source):
        block, slot, experts, sends = picks(i, number)

        @pl.when(i >= 2)
        def _():
            for send in sends[1:]:
                send.wait_send()

        select = one_hot(pos_ref, experts, block, capacity)
        picked[slot, number] = jnp.dot(select, source[...], preferred_element_type=f32).astype(low)
        for stream in range(2):

            @pl.when(unit(i)[1] == stream)
            def _():
                for send in picks(i, number, rows_refs[stream])[3]:
                    send.start()

    def wait_own(i, number):
        picks(i, number)[3][0].wait()

    def pair(c):
        plane = plane_of(lax.div(c, 4))
        j = lax.rem(c, 4)
        owner = (
            e + lax.rem(j, 2) * (here.x_same - e) + lax.div(j, 2) * (here.y_same - e)
        )
        first = plane * PLANE + owner
        at = owner * LINE + plane
        owners = (owner, owner + here.sib - e)
        return j, first, first + here.sib - e, (at, at + (here.sib - e) * LINE, plane, owners)

    def takes(c):
        _, first, second, _ = pair(c)
        slot = lax.rem(c, 2)
        return [
            pltpu.make_async_copy(
                rows_refs[stream].at[block],
                taken.at[slot, stream, pl.ds(number * capacity, capacity)],
                taken_sem.at[slot, stream, number],
            )
            for stream in range(2)
            for number, block in enumerate((first, second))
        ]

    def take(c):
        j, first, second, _ = pair(c)

        def wait_rows(block, half):
            for stream in range(2):
                for part in range(2):
                    wait_for(
                        rows_refs[stream].at[block, :, part_columns(half, part)],
                        row_recv.at[stream, block, half, part],
                    )

        for half in range(2):
            wait_rows(second, half)

        @pl.when((j == 2) | (j == 3))
        def _():
            wait_rows(first, 0)

        @pl.when((j == 1) | (j == 3))
        def _():
            wait_rows(first, 1)

        for copy in takes(c):
            copy.start()

    def puts(c):
        _, first, second, out_at = pair(c)
        out = []
        for number, block in enumerate((first, second)):
            at = pl.ds(number * capacity, capacity)
            for kind, (held, goal) in enumerate(
                (
                    (out_held.at[:, pl.ds(0, FIRST_COLUMNS)], out_ref),
                    (
                        out_held.at[:, pl.ds(FIRST_COLUMNS, MODEL_WIDTH - FIRST_COLUMNS)],
                        out_second_ref,
                    ),
                    (back_held, back_ref),
                    (act_held, act_ref),
                    (gate_held, gate_low_ref),
                    (up_held, up_low_ref),
                )
            ):
                to = out_at[number] if kind < 2 else block
                out.append(
                    pltpu.make_async_copy(held.at[at], goal.at[to], put_sem.at[kind, number])
                )
        return out

    def compute(c):
        for copy in takes(c):
            copy.wait()

        @pl.when(c > 0)
        def _():
            for copy in puts(c - 1):
                copy.wait()

        slot = lax.rem(c, 2)
        _, first, second, (_, _, plane, owners) = pair(c)
        slots = lax.broadcasted_iota(jnp.int32, (capacity, DEVICE_TOKENS), 0)
        chosen = [slots == pos_ref[e, pl.ds(block, 1), :] for block in (first, second)]
        gates = jnp.concatenate(
            [
                jnp.sum(
                    jnp.where(mask, gates_here[plane, owner], 0.0), axis=1, keepdims=True
                )
                for mask, owner in zip(chosen, owners)
            ],
            axis=0,
        )
        rows = taken[slot, 0]
        gate_part = jnp.dot(rows, w_gate_ref[...], preferred_element_type=f32)
        up_part = jnp.dot(rows, w_up_ref[...], preferred_element_type=f32)
        sigmoid = 1.0 / (1.0 + jnp.exp(-gate_part))
        silu = gate_part * sigmoid
        act_low = (silu * up_part).astype(low)
        pull = across(taken[slot, 1], w_down_ref[...], (1, 1))
        act = act_low.astype(f32)
        row_grad = jnp.sum(act * pull, axis=1, keepdims=True)
        for number, owner in enumerate(owners):
            mine = row_grad[number * capacity : (number + 1) * capacity]
            gate_grad_ref[plane, owner] = jnp.sum(
                jnp.where(chosen[number], mine, 0.0), axis=0, keepdims=True
            )
        act_held[...] = (act * gates).astype(low)
        pull = pull * gates
        gate_low = (pull * up_part * (sigmoid * (1.0 + gate_part * (1.0 - sigmoid)))).astype(low)
        up_low = (pull * silu).astype(low)
        gate_held[...] = gate_low
        up_held[...] = up_low
        out_held[...] = (
            jnp.dot(act_low, w_down_ref[...], preferred_element_type=f32) * gates
        ).astype(low)
        back_held[...] = (
            across(gate_low, w_gate_ref[...], (1, 1)) + across(up_low, w_up_ref[...], (1, 1))
        ).astype(low)
        for copy in puts(c):
            copy.start()

    def step(i, carry):
        @pl.when((i > 0) & (i <= UNITS))
        def _():
            wait_own(i - 1, 0)
            wait_own(i - 1, 1)

        @pl.when(i < UNITS)
        def _():
            for half in range(2):
                wait_for(near.at[half], near_sem.at[half])
                pick(i, half, near.at[half])

        @pl.when((i > 0) & (i <= UNITS))
        def _():
            for half in range(2):
                wait_for(side.at[half], side_sem.at[half])
                pick(i - 1, 2 + half, side.at[half])

        @pl.when(i < UNITS - 1)
        def _():
            arrive(i + 1)

        @pl.when(i < UNITS)
        def _():
            arrive_side(i)

        @pl.when(i == 1)
        def _():
            spread_gates()

        @pl.when(i == LAG)
        def _():
            wait_gates()

        @pl.when(i >= LAG)
        def _():
            @pl.when(lax.rem(i - LAG, 4) == 0)
            def _():
                take(i - LAG)

            compute(i - LAG)

        @pl.when((i > 0) & (i <= UNITS))
        def _():
            wait_own(i - 1, 2)
            wait_own(i - 1, 3)

        @pl.when((i >= LAG) & (lax.rem(i - LAG, 4) != 3))
        def _():
            take(i - (LAG - 1))

        for first_step, last_step, ahead in ((1, 4, 3), (2, 5, 6), (5, 8, 7)):

            @pl.when(
                (i >= first_step)
                & (i <= last_step)
                & jnp.logical_not(at_an_end)
                & jnp.logical_not(early(i + ahead))
            )
            def _():
                pass_on(i + ahead)

        @pl.when(i == 1)
        def _():
            pass_side_on(i + 2)

        for at_step, ahead in ((5, 2), (6, 5), (10, 5)):

            @pl.when((i == at_step) & jnp.logical_not(at_an_end))
            def _():
                pass_side_on(i + ahead)

        return carry

    for i in (0, 1, 3):
        pass_on(jnp.int32(i))
    for send in denses(jnp.int32(3)):
        send.start()
    arrive(jnp.int32(0))
    lax.fori_loop(0, UNITS + LAG, step, 0)
    for copy in puts(UNITS - 1):
        copy.wait()
    for move in gate_moves + gate_moves_on:
        move.wait_send()
    for i in (UNITS - 2, UNITS - 1):
        for number in range(4):
            for send in picks(jnp.int32(i), number)[3][1:]:
                send.wait_send()

    def drain(i, carry):
        @pl.when(jnp.logical_not(early(i)))
        def _():
            along(i, forwards(i), lambda send: send.wait_send())

            @pl.when(jnp.logical_not(side_first(i)) | (i == 3))
            def _():
                for send in denses(i):
                    send.wait_send()

        @pl.when(side_first(i))
        def _():
            along(i, side_forwards(i), lambda send: send.wait_send())

        return carry

    lax.fori_loop(0, UNITS, drain, 0)


def dispatch_and_expert(
    routed,
    cotangent,
    early_line,
    early_sides,
    positions,
    gates,
    w_gate,
    w_up,
    w_down,
    capacity,
    collective_id,
):
    low, f32 = jnp.bfloat16, jnp.float32
    blocks = LINE * PLANE
    dma = pltpu.SemaphoreType.DMA
    wide = jax.ShapeDtypeStruct((blocks, capacity, MODEL_WIDTH), low)
    narrow = jax.ShapeDtypeStruct((blocks, capacity, w_gate.shape[1]), low)
    landing = jax.ShapeDtypeStruct((2, 2, LINE, 2, DEVICE_TOKENS, PART), low)
    vmem = pl.BlockSpec(memory_space=pltpu.VMEM)
    anywhere = pl.BlockSpec(memory_space=pl.ANY)
    chunk = CHUNK * capacity
    return pl.pallas_call(
        expert_kernel,
        out_shape=[
            wide,
            wide,
            jax.ShapeDtypeStruct((blocks, capacity, FIRST_COLUMNS), low),
            jax.ShapeDtypeStruct((blocks, capacity, MODEL_WIDTH - FIRST_COLUMNS), low),
            wide,
            narrow,
            narrow,
            narrow,
            jax.ShapeDtypeStruct(GATE_SHAPE, f32),
            landing,
            landing,
        ],
        in_specs=[vmem] * 5 + [anywhere] * 5,
        out_specs=[anywhere] * 8 + [vmem] + [anywhere] * 2,
        scratch_shapes=[
            pltpu.VMEM((2, DEVICE_TOKENS, MODEL_WIDTH), low),
            pltpu.VMEM((2, DEVICE_TOKENS, PART), low),
            pltpu.VMEM((2, DEVICE_TOKENS, PART), low),
            pltpu.VMEM(GATE_SHAPE, f32),
            pltpu.VMEM(GATE_SHAPE, f32),
            pltpu.VMEM((2, 4, 4 * capacity, PART), low),
            pltpu.VMEM((2, 2, chunk, MODEL_WIDTH), low),
            pltpu.VMEM((chunk, MODEL_WIDTH), low),
            pltpu.VMEM((chunk, MODEL_WIDTH), low),
            pltpu.VMEM((chunk, w_gate.shape[1]), low),
            pltpu.VMEM((chunk, w_gate.shape[1]), low),
            pltpu.VMEM((chunk, w_gate.shape[1]), low),
            dma((UNITS, 2, 2)),
            dma((2, 2, LINE, 2)),
            dma((UNITS, 2)),
            dma((2, 2, LINE, 2)),
            dma((LINE, 2, 2)),
            dma((2, 4, 4)),
            dma((2, blocks, 2, 2)),
            dma((2, 4)),
            dma((2,)),
            dma((2,)),
            dma((2, 2, 2)),
            dma((6, 2)),
            dma((LINE,)),
            dma((LINE,)),
            dma((PLANE,)),
            dma((PLANE,)),
        ],
        compiler_params=pltpu.CompilerParams(
            collective_id=collective_id, has_side_effects=True, vmem_limit_bytes=60 * 2**20
        ),
    )(positions, gates, w_gate, w_up, w_down, routed, cotangent, early_line, *early_sides)[:9]


def on_device(
    tokens,
    segments,
    routes,
    w_query,
    key_projection,
    value_projection,
    w_out,
    w_router,
    gain_attn,
    gain_ffn,
    gain_query,
    key_head_gain,
    w_gate,
    w_up,
    w_down,
    cotangent,
):
    f32 = jnp.float32
    brain_float = jnp.bfloat16
    sequence_length = tokens.shape[0]
    planes = lax.axis_size("fsdp")
    experts = planes * lax.axis_size("expert")
    capacity = 5 * DEVICE_TOKENS * TOP // (4 * experts)
    expert_ids = jnp.arange(experts, dtype=jnp.int32)
    my_expert = lax.axis_index("fsdp") * lax.axis_size("expert") + lax.axis_index("expert")
    in_blocks = (planes, experts) == (LINE, LINE * PLANE)

    small = (w_router, gain_attn, gain_ffn, gain_query, key_head_gain)
    small_sizes = [array.size for array in small]
    local_qkv = jnp.concatenate([w_query, key_projection, value_projection], axis=1)
    small_flat = jnp.concatenate([array.reshape(-1) for array in small])
    if in_blocks:
        width = -(-small_flat.size // (16 * 128)) * 128
        small_flat = jnp.pad(small_flat, (0, 16 * width - small_flat.size))
        cot_front = jnp.concatenate(
            [cotangent[:, :PART], cotangent[:, 2 * PART : 3 * PART]], axis=1
        )
        full_qkv, full_out, small_all, cot_line, routes_all = gather_all(
            (local_qkv, w_out), small_flat.reshape(16, width), cot_front, routes.T, 3
        )
        cot_line = cot_line.reshape(planes, sequence_length, 2 * PART)
        cot_sides = [
            lax.ppermute(
                cot_line[:, :, half * PART : (half + 1) * PART],
                "expert",
                [(device, device ^ (2 << half)) for device in range(PLANE)],
            )
            for half in range(2)
        ]
        small_all = small_all.reshape(planes, -1)
        routes_all = routes_all.reshape(experts, TOP, sequence_length)
    else:
        full_qkv = gather_shards(local_qkv)
        full_out = gather_shards(w_out)
        small_all = lax.all_gather(small_flat, "fsdp", axis=0)
    small_parts = []
    offset = 0
    for array, size in zip(small, small_sizes):
        part = small_all[:, offset : offset + size]
        small_parts.append(part.reshape((planes * array.shape[0],) + array.shape[1:]))
        offset += size
    full_router, attn_gain, ffn_gain, query_gain, key_gain = small_parts

    if in_blocks:
        plane_experts = lax.axis_index("fsdp") * PLANE + jnp.arange(PLANE, dtype=jnp.int32)
        plane_hits = jnp.any(routes_all[None] == plane_experts[:, None, None, None], axis=2)
        positions = ranks(plane_hits)
    else:
        hits = jnp.any(routes[None, :, :] == expert_ids[:, None, None], axis=-1)
        select = places(hits, capacity)
        cot_rows = jnp.einsum("brt,td->brd", select, cotangent, preferred_element_type=f32)
        cot_rows = lax.all_to_all(cot_rows.astype(brain_float), BOTH, 0, 0, tiled=True)

    inputs = tokens.astype(f32)
    normalized, norm_attn_back = jax.vjp(root_mean_norm, inputs, attn_gain.astype(f32))
    normed_low = normalized.astype(brain_float)
    qkv_raw = jnp.dot(normed_low, full_qkv, preferred_element_type=f32)
    cosine, sine = rope_tables(sequence_length, HEAD_SIZE)
    head_gains = (query_gain.astype(f32)[None, :], key_gain.astype(f32)[None, :])
    mixed_low, query_rot, key_rot, value_low, totals = attention(
        qkv_raw, segments, cosine, sine, *head_gains
    )
    hidden = inputs + jnp.dot(mixed_low, full_out, preferred_element_type=f32)
    routed, norm_ffn_back = jax.vjp(root_mean_norm, hidden, ffn_gain.astype(f32))
    routed_low = routed.astype(brain_float)
    logits = jnp.dot(routed_low, full_router, preferred_element_type=f32)
    chosen_mask = jnp.any(routes[:, :, None] == expert_ids[None, None, :], axis=1)

    def gating(logit_in):
        softmax_probs = jax.nn.softmax(logit_in, axis=-1)
        chosen = jnp.where(chosen_mask, softmax_probs, 0.0)
        return chosen / jnp.sum(chosen, axis=-1, keepdims=True)

    gates, gating_back = jax.vjp(gating, logits)
    flat = (experts * capacity, MODEL_WIDTH)
    if in_blocks:
        (
            rows,
            cot_rows,
            out_rows,
            out_second,
            rows_grad,
            act_low,
            gate_low,
            up_low,
            gate_grad,
        ) = dispatch_and_expert(
            routed_low,
            cotangent,
            cot_line,
            cot_sides,
            positions,
            gates.T.reshape(GATE_SHAPE),
            w_gate[0],
            w_up[0],
            w_down[0],
            capacity,
            1,
        )
    else:
        rows = jnp.einsum("brt,td->brd", select, routed_low, preferred_element_type=f32)
        rows = lax.all_to_all(rows.astype(brain_float), BOTH, 0, 0, tiled=True)
        here = lax.all_to_all(select, BOTH, 0, 0, tiled=True)
        gates_here = lax.all_to_all(gates.T, BOTH, 0, 0, tiled=True)
        row_gates = jnp.sum(here.astype(f32) * gates_here[:, None, :], axis=-1)
        (
            out_rows,
            rows_grad,
            row_gate_grad,
            gate_weight_grad,
            up_weight_grad,
            down_weight_grad,
        ) = expert_layer(
            rows.reshape(flat),
            cot_rows.reshape(flat),
            row_gates.reshape(-1),
            w_gate[0],
            w_up[0],
            w_down[0],
        )
        row_gate_grad = row_gate_grad.reshape(experts, capacity, 1)
        gate_grad = jnp.sum(here.astype(f32) * row_gate_grad, axis=1)

    def exchange_back(block, select_here):
        block = block.reshape(experts, capacity, MODEL_WIDTH)
        block = lax.all_to_all(block, BOTH, 0, 0, tiled=True)
        return jnp.einsum("brt,brd->td", select_here, block, preferred_element_type=f32)

    if in_blocks:
        routed_grad, gate_grad = combine(
            rows_grad.reshape(experts, capacity, MODEL_WIDTH), positions, gate_grad, 2
        )
        gate_grad = gate_grad.reshape(experts, sequence_length).T
        (
            out_rows,
            rows,
            cot_rows,
            act_low,
            gate_low,
            up_low,
            routed_grad,
        ) = lax.optimization_barrier(
            (out_rows, rows, cot_rows, act_low, gate_low, up_low, routed_grad)
        )

        def in_plane(block):
            return lax.all_to_all(
                block.reshape(PLANE, LINE, capacity, -1), "expert", 0, 0, tiled=True
            )

        gate_weight_grad, up_weight_grad = routed_weight_grads(
            rows.reshape(flat), gate_low.reshape(flat[0], -1), up_low.reshape(flat[0], -1)
        )

        def in_plane(block):
            return lax.all_to_all(
                block.reshape(PLANE, LINE, capacity, -1), "expert", 0, 0, tiled=True
            )

        returned = in_plane(out_rows)
        line_positions = lax.dynamic_index_in_dim(
            positions.reshape(PLANE, LINE, PLANE, sequence_length),
            lax.axis_index("expert"),
            axis=2,
            keepdims=False,
        )
        slots = jnp.arange(capacity, dtype=jnp.int32)
        line_select = (line_positions[:, :, None, :] == slots[:, None]).astype(brain_float)

        def sum_along(block):
            sums = jnp.einsum("ezct,ezcd->ztd", line_select, block, preferred_element_type=f32)
            sums = sums.astype(brain_float).reshape(-1, block.shape[-1])
            return lax.psum_scatter(sums, "fsdp", scatter_dimension=0, tiled=True), sums

    else:
        gate_grad = lax.all_to_all(gate_grad, BOTH, 0, 0, tiled=True).T
        routed_grad = exchange_back(rows_grad, select)
        result = hidden + exchange_back(out_rows, select)
    upstream = cotangent.astype(f32)
    logit_low = gating_back(gate_grad)[0].astype(brain_float)
    routed_grad = routed_grad + jnp.einsum(
        "se,de->sd", logit_low, full_router, preferred_element_type=f32
    )
    router_grad = jnp.einsum("sd,se->de", routed_low, logit_low, preferred_element_type=f32)
    hidden_grad, ffn_gain_grad = norm_ffn_back(routed_grad)
    hidden_grad = hidden_grad + upstream
    hidden_low = hidden_grad.astype(brain_float)
    mixture_gradient = jnp.einsum(
        "sd,ad->sa", hidden_low, full_out, preferred_element_type=f32
    ).astype(brain_float)
    query_pre, key_pre, value_pre, gain_grads = attention_back(
        qkv_raw,
        query_rot,
        key_rot,
        value_low,
        mixture_gradient,
        totals,
        segments,
        cosine,
        sine,
        *head_gains,
    )
    if in_blocks:
        (
            returned,
            out_second,
            query_pre,
            gate_weight_grad,
            up_weight_grad,
            cot_rows,
            act_low,
            mixed_low,
        ) = lax.optimization_barrier(
            (
                returned,
                out_second,
                query_pre,
                gate_weight_grad,
                up_weight_grad,
                cot_rows,
                act_low,
                mixed_low,
            )
        )
        down_weight_grad = down_weight_grads(
            cot_rows.reshape(flat), act_low.reshape(flat[0], -1)
        )
        result_first, _ = sum_along(returned)
        returned = in_plane(out_second)
    out_grad = jnp.einsum("sa,sd->ad", mixed_low, hidden_low, preferred_element_type=f32)
    qkv_pre = jnp.concatenate([query_pre, key_pre, value_pre], axis=1)
    qkv_weight_grad = jnp.einsum("sd,sa->da", normed_low, qkv_pre, preferred_element_type=f32)
    normed_grad = jnp.einsum("sa,da->sd", qkv_pre, full_qkv, preferred_element_type=f32)
    input_grad, attn_gain_grad = norm_attn_back(normed_grad)
    input_grad = (input_grad + hidden_grad).astype(brain_float)
    small_grads = [
        grad.reshape(planes, -1).astype(brain_float)
        for grad in (router_grad, attn_gain_grad, ffn_gain_grad, gain_grads[0], gain_grads[1])
    ]
    small_grads = jnp.concatenate(small_grads, axis=1)
    if in_blocks:
        lanes = 128
        width = -(-small_grads.shape[1] // (PLANE * 32 * lanes)) * (PLANE * 32 * lanes)
        small_grads = jnp.pad(small_grads, ((0, 0), (0, width - small_grads.shape[1])))
        qkv_low = qkv_weight_grad.astype(brain_float)
        out_low = out_grad.astype(brain_float)
        (
            returned,
            qkv_low,
            out_low,
            input_grad,
            gate_weight_grad,
            up_weight_grad,
            down_weight_grad,
        ) = lax.optimization_barrier(
            (
                returned,
                qkv_low,
                out_low,
                input_grad,
                gate_weight_grad,
                up_weight_grad,
                down_weight_grad,
            )
        )
        result_second, expert_sums = sum_along(returned)
        qkv_low, expert_sums = lax.optimization_barrier((qkv_low, expert_sums))
        qkv_sum, out_sum, small_sums = reduce_all(
            (qkv_low, out_low, small_grads.reshape(-1, lanes)), 4
        )
        qkv_sum, out_sum = qkv_sum.astype(f32), out_sum.astype(f32)
        result = hidden + jnp.concatenate([result_first, result_second], axis=1).astype(f32)
        small_sums = small_sums.reshape(-1).astype(f32)
    else:
        qkv_sum = scatter_sums(qkv_weight_grad.astype(brain_float))
        out_sum = scatter_sums(out_grad.astype(brain_float))
        small_sums = lax.psum(
            lax.psum_scatter(small_grads, "fsdp", scatter_dimension=0, tiled=True), "expert"
        ).astype(f32)[0]
    query_width = QUERY_HEADS * HEAD_SIZE
    key_width = query_width + KEY_VALUE_HEADS * HEAD_SIZE
    summed = [
        qkv_sum[:, :query_width],
        qkv_sum[:, query_width:key_width],
        qkv_sum[:, key_width:],
        out_sum,
    ]
    offset = 0
    for array, size in zip(small, small_sizes):
        summed.append(small_sums[offset : offset + size].reshape(array.shape))
        offset += size
    return (
        (result.astype(brain_float), input_grad)
        + tuple(summed)
        + (gate_weight_grad[None], up_weight_grad[None], down_weight_grad[None])
    )


def solution(mesh):
    in_specs = (
        P(("fsdp", "expert"), None),
        P(("fsdp", "expert"), None),
        P(("fsdp", "expert"), None),
        P("fsdp", None),
        P("fsdp", None),
        P("fsdp", None),
        P("fsdp", None),
        P("fsdp", None),
        P("fsdp"),
        P("fsdp"),
        P("fsdp"),
        P("fsdp"),
        P(("fsdp", "expert"), None, None),
        P(("fsdp", "expert"), None, None),
        P(("fsdp", "expert"), None, None),
        P(("fsdp", "expert"), None),
    )
    out_specs = (
        P(("fsdp", "expert"), None),
        P(("fsdp", "expert"), None),
        P("fsdp", None),
        P("fsdp", None),
        P("fsdp", None),
        P("fsdp", None),
        P("fsdp", None),
        P("fsdp"),
        P("fsdp"),
        P("fsdp"),
        P("fsdp"),
        P(("fsdp", "expert"), None, None),
        P(("fsdp", "expert"), None, None),
        P(("fsdp", "expert"), None, None),
    )
    return jax.shard_map(
        on_device, mesh=mesh, in_specs=in_specs, out_specs=out_specs, check_vma=False
    )
```
